32 devices in a mesh: half: 2 (over core), dp: 8 (over z, x), mp: 2 (over y).
Axes of the slice: x: 2, y: 2, z: 4, core: 2. Of those that a mesh axis runs over, the one named last changes fastest.
Arguments:
- tokens: bfloat16 [2, 16384, 768], P('half', ('dp', 'mp')), may hold values from -6 to 6
- norm_gains: float32 [2, 2, 768], P('half'), may hold values from 0.5 to 1.5
- qkv_w: bfloat16 [2, 768, 3, 768], P('half', None, None, 'mp'), may hold values from -0.21875 to 0.21875
- out_w: bfloat16 [2, 768, 768], P('half', None, 'mp'), may hold values from -0.875 to 0.875
- up_w: bfloat16 [2, 768, 3072], P('half', None, 'mp'), may hold values from -0.21875 to 0.21875
- down_w: bfloat16 [2, 768, 3072], P('half', None, 'mp'), may hold values from -0.109375 to 0.109375
- memory: bfloat16 [2, 4096, 4, 768], P('half', 'dp'), may hold values from -12 to 12
- memory_ids: int32 [256, 10], P(('dp', 'mp')), may hold values from 0 to 4095, as said below
- counts: int32 [256], P(('dp', 'mp')), may hold values from 1 to 10, 1536 in all
- prefix_mask: int32 [256, 20], P(('dp', 'mp')), may hold values 0 or 1
- cotangent: bfloat16 [2, 16384, 768], P('half', ('dp', 'mp')), may hold values from -6 to 6
Outputs:
- activations: bfloat16 [2, 16384, 768], P('half', ('dp', 'mp'))
- input_grad: float32 [2, 16384, 768], P('half', ('dp', 'mp'))
- score_grads: float32 [256, 10], P(('dp', 'mp'))
- gain_grads: float32 [2, 2, 768], P('half')
- qkv_grads: float32 [2, 768, 3, 768], P('half', 'dp', None, 'mp')
- out_grads: float32 [2, 768, 768], P('half', 'dp', 'mp')
- up_grads: float32 [2, 768, 3072], P('half', 'dp', 'mp')
- down_grads: float32 [2, 768, 3072], P('half', 'dp', 'mp')
The draws below stay inside these ranges and needn't reach their ends.
Inputs may be any that keep to these rules, and one draw needn't show every extreme that they name: memory_ids[q, j] // 512 = (i + t * 10 + j) mod 8, where q is the t-th of the 16 questions held by a device whose dp index is i.
All inputs are finite; a program needn't handle non-finite values. No bound on the sum of `counts` or of `prefix_mask` on one device may be relied on, other than what follows from the above.
Results may differ from the reference program's by a relative error of at most 0.017.
Values may be sent and summed in bfloat16 or wider, within the bound.
No kernel may reach another device: no remote copies, remote signals or barrier semaphores. Data moves between devices by JAX's collectives and lax.ppermute only.
A program may use at most 320 MiB of HBM per device.

```python
import math
import jax
import jax.numpy as jnp
import numpy as np
from jax import lax

D = 768
HEADS = 12
HDIM = 64
FF = 3072
QLEN = 64
KMAX = 10
MEM_DEV = 512
HD = 768
TOKENS = 16384
QUESTIONS = 256
QD = 16
MEM = 4096
SHARDS = 8
SPLIT = 2


def draw_memory_ids(key, part):
    question = jnp.arange(QUESTIONS)
    position = question % QD
    shard_of = question // QD // SPLIT
    slot_order = position[:, None] * KMAX + jnp.arange(KMAX)[None, :]
    owner_shard = (shard_of[:, None] + slot_order) % SHARDS
    offset = jax.random.randint(key, (QUESTIONS, KMAX), 0, MEM_DEV)
    first_slot = (position[:, None] == 0) & (jnp.arange(KMAX)[None, :] == 0)
    offset = jnp.where(first_slot & (shard_of[:, None] == SHARDS - 1), MEM_DEV - 1, offset)
    offset = jnp.where(first_slot & (shard_of[:, None] == 0), 0, offset)
    return (owner_shard * MEM_DEV + offset).astype(jnp.int32)


def place_ends(values, key, low, largest):
    extent = values.shape
    index_at = [jax.random.randint(jax.random.fold_in(key, axis), (), 0, extent[axis]) for axis in range(len(extent))]
    values = values.at[tuple(index_at)].set(low)
    longest = extent.index(max(extent))
    index_at[longest] = (index_at[longest] + 1) % extent[longest]
    return values.at[tuple(index_at)].set(largest)


def steps_of(own_key, extent, cuts, smallest, high):
    loudness, own = 1.0, jax.random.fold_in(own_key, 6)
    for dim, blocks in cuts:
        steps = jnp.exp(jax.random.uniform(jax.random.fold_in(own, dim), (blocks,), jnp.float32, smallest / len(cuts), high / len(cuts)))
        loudness = loudness * jnp.repeat(steps, extent[dim] // blocks).reshape([-1 if axis == dim else 1 for axis in range(len(extent))])
    return loudness


def profile(amount, total, bound, lean):
    portions = [(1 << 20) // math.isqrt(grade ** lean) + 1 for grade in range(2, amount + 1)]
    rest, given = total - bound - (amount - 1), [1] * (amount - 1)
    while rest > 0:
        movable = [i for i in range(amount - 1) if given[i] < bound]
        mass, remaining = sum([portions[i] for i in movable]), rest
        for i in movable:
            extra = min(bound - given[i], max(1, remaining * portions[i] // mass), rest)
            given[i] = given[i] + extra
            rest = rest - extra
    return np.array([bound] + given)


def uneven(rng, count, total, limit, lean):
    if count == 2:
        one = jax.random.randint(rng, (), max(1, total - limit), min(limit, total - 1) + 1)
        return jnp.stack([one, total - one])
    sizes = jnp.asarray(profile(count, total, limit, lean), jnp.int32)
    pairs = (count - 1) // 2
    source_of, taker = sizes[1:1 + 2 * pairs:2], sizes[2:2 + 2 * pairs:2]
    room = jnp.minimum(source_of - 1, limit - taker)
    passed = jax.random.randint(jax.random.fold_in(rng, 1), (pairs,), 0, 1 << 20) % (room + 1)
    sizes = sizes.at[1:1 + 2 * pairs:2].set(source_of - passed).at[2:2 + 2 * pairs:2].set(taker + passed)
    return sizes[jax.random.permutation(jax.random.fold_in(rng, 2), count)]


def normal_values(key, shape, spread, most, split=(), dtype=jnp.bfloat16):
    level = steps_of(key, shape, split, -0.22, 0.18) if split else 1.0
    values = jax.random.normal(key, shape, jnp.float32) * spread * level
    return jnp.minimum(jnp.maximum(values, -most), most).astype(dtype)


def setup_inputs(seed: int = 0) -> dict:
    streams_of = jax.random.split(jax.random.key(seed), 12)
    return {
        "tokens": normal_values(streams_of[0], (2, TOKENS, D), 1.0, 6.0, ((0, 2), (1, 16))),
        "norm_gains": jnp.clip(1.0 + 0.1 * jax.random.normal(streams_of[1], (2, 2, D), jnp.float32), 0.5, 1.5),
        "qkv_w": normal_values(streams_of[2], (2, D, 3, HD), D ** -0.5, 0.21875, ((0, 2), (3, 2))),
        "out_w": normal_values(streams_of[3], (2, D, HD), (HD // 16) ** -0.5, 0.875, ((0, 2), (2, 2))),
        "up_w": normal_values(streams_of[4], (2, D, FF), D ** -0.5, 0.21875, ((0, 2), (2, 2))),
        "down_w": normal_values(streams_of[5], (2, D, FF), FF ** -0.5, 0.109375, ((0, 2), (2, 2))),
        "memory": normal_values(streams_of[6], (2, MEM, 4, D), 2.0, 12.0, ((0, 2), (1, 8))),
        "memory_ids": draw_memory_ids(jax.random.fold_in(streams_of[11], 71), 0),
        "counts": uneven(streams_of[8], QUESTIONS, 6 * QUESTIONS, KMAX, 1).astype(jnp.int32),
        "prefix_mask": place_ends((jax.random.randint(streams_of[9], (QUESTIONS, 2 * KMAX), 0, 4) < 3).astype(jnp.int32), jax.random.fold_in(streams_of[9], 1), 0, 1),
        "cotangent": normal_values(streams_of[10], (2, TOKENS, D), 1.0, 6.0, ((0, 2), (1, 16))),
    }


NORM_EPS = 1e-06
MASKED_LOGIT = -1e+30
HIGHEST_MODE = lax.Precision.HIGHEST

@jax.custom_vjp
def low(v):
    return lax.optimization_barrier(v.astype(jnp.bfloat16)).astype(jnp.float32)

@jax.custom_vjp
def low_back(v):
    return v

def low_keep(v):
    return (low(v), None)

def low_pass(kept, grad):
    return (grad,)

def back_keep(v):
    return (v, None)

def back_low(kept, grad):
    return (low(grad),)
low.defvjp(low_keep, low_pass)
low_back.defvjp(back_keep, back_low)

def rms_norm(row_block, gain_vec):
    return row_block * lax.rsqrt(lax.optimization_barrier(jnp.mean(row_block * row_block, axis=-1, keepdims=True)) + NORM_EPS) * gain_vec

def gelu_tanh(pre_act):
    return jax.nn.gelu(pre_act, approximate=True)

def attend(queries, keys_all, values_all, bias_block, valid_block):
    logits = jnp.einsum('nthe,nshe->nhts', queries, keys_all, precision=HIGHEST_MODE) * HDIM ** (-0.5)
    if bias_block is not None:
        logits = jnp.where(valid_block[:, None, None, :], logits + bias_block[:, None, None, :], MASKED_LOGIT)
    probs = low(jax.nn.softmax(logits, axis=-1))
    return jnp.einsum('nhts,nshe->nthe', probs, values_all, precision=HIGHEST_MODE)

def encoder_layer(row_block, gain_pair, qkv_mat, out_mat, up_mat, down_mat, prefix_set):
    count_q = row_block.shape[0] // QLEN
    normed = low(rms_norm(row_block, gain_pair[0]))
    projected = low(low_back(jnp.einsum('td,dch->tch', normed, qkv_mat, precision=HIGHEST_MODE)))
    queries = projected[:, 0].reshape(count_q, QLEN, HEADS, HDIM)
    keys_own = projected[:, 1].reshape(count_q, QLEN, HEADS, HDIM)
    values_own = projected[:, 2].reshape(count_q, QLEN, HEADS, HDIM)
    if prefix_set is None:
        mixed_heads = attend(queries, keys_own, values_own, None, None)
    else:
        pref_keys, pref_values, bias_block, valid_block = prefix_set
        mixed_heads = attend(queries, jnp.concatenate([keys_own, pref_keys], axis=1), jnp.concatenate([values_own, pref_values], axis=1), bias_block, valid_block)
    mixed_heads = low(low_back(mixed_heads.reshape(count_q * QLEN, HEADS * HDIM)))
    attn_out = low_back(jnp.einsum('th,dh->td', mixed_heads, out_mat, precision=HIGHEST_MODE))
    residual = row_block + attn_out
    normed_two = low(rms_norm(residual, gain_pair[1]))
    hidden_pre = low_back(jnp.einsum('td,df->tf', normed_two, up_mat, precision=HIGHEST_MODE))
    hidden = low(gelu_tanh(hidden_pre))
    return residual + low_back(jnp.einsum('tf,df->td', hidden, down_mat, precision=HIGHEST_MODE))

def reference(tokens, norm_gains, qkv_w, out_w, up_w, down_w, memory, memory_ids, counts, prefix_mask, cotangent):
    block_q = 64
    n_blocks = QUESTIONS // block_q
    found_rows = memory.astype(jnp.float32)[:, memory_ids]
    slot_valid = ((jnp.arange(KMAX)[None, :] < counts[:, None])[:, :, None] & (prefix_mask.reshape(QUESTIONS, KMAX, 2) == 1)).reshape(QUESTIONS, 2 * KMAX)
    full_valid = jnp.concatenate([jnp.ones((QUESTIONS, QLEN), jnp.bool_), slot_valid], axis=1)

    def forward(inputs, gain_set, qkv_set, out_set, up_set, down_set, score_shift):

        def key_block(pair_in):
            row_block, key_rows = pair_in
            result = encoder_layer(row_block, gain_set[0], qkv_set[0], out_set[0], up_set[0], down_set[0], None)
            pooled = lax.optimization_barrier(jnp.mean(result.reshape(block_q, 4, QLEN // 4, D), axis=2))
            scores = jnp.einsum('ncd,njcd->nj', pooled, key_rows, precision=HIGHEST_MODE) * (4 * D) ** (-0.5)
            return (result, scores)
        key_out, scores = lax.map(jax.checkpoint(key_block), (inputs[0].reshape(n_blocks, block_q * QLEN, D), found_rows[0].reshape(n_blocks, block_q, KMAX, 4, D)))
        sent_scores = low(low_back(scores.reshape(QUESTIONS, KMAX) + score_shift))
        bias_full = jnp.concatenate([jnp.zeros((QUESTIONS, QLEN), jnp.float32), jnp.repeat(sent_scores, 2, axis=1)], axis=1)

        def join_block(group_in):
            row_block, pref_rows, bias_block, valid_block = group_in
            prefix_set = (pref_rows[:, :, 0:2].reshape(block_q, 2 * KMAX, HEADS, HDIM), pref_rows[:, :, 2:4].reshape(block_q, 2 * KMAX, HEADS, HDIM), bias_block, valid_block)
            return encoder_layer(row_block, gain_set[1], qkv_set[1], out_set[1], up_set[1], down_set[1], prefix_set)
        join_out = lax.map(jax.checkpoint(join_block), (inputs[1].reshape(n_blocks, block_q * QLEN, D), found_rows[1].reshape(n_blocks, block_q, KMAX, 4, D), bias_full.reshape(n_blocks, block_q, QLEN + 2 * KMAX), full_valid.reshape(n_blocks, block_q, QLEN + 2 * KMAX)))
        return jnp.stack([key_out.reshape(TOKENS, D), join_out.reshape(TOKENS, D)])
    outputs, pullback = jax.vjp(forward, tokens.astype(jnp.float32), norm_gains, qkv_w.astype(jnp.float32), out_w.astype(jnp.float32), up_w.astype(jnp.float32), down_w.astype(jnp.float32), jnp.zeros((QUESTIONS, KMAX), jnp.float32))
    gradients = pullback(cotangent.astype(jnp.float32))
    return (outputs.astype(jnp.bfloat16), gradients[0], gradients[6], gradients[1], gradients[2], gradients[3], gradients[4], gradients[5])
```

```python
import functools

import jax
import jax.numpy as jnp
from jax import lax
from jax.experimental import pallas as pl
from jax.experimental.pallas import tpu as pltpu
from jax.sharding import PartitionSpec as P

HDIM = 64
QLEN = 64
RUN = 16
LANES = 128
NORM_EPS = 1e-06
MASKED = -1e30
HIGHEST = lax.Precision.HIGHEST
F32 = jnp.float32
BF16 = jnp.bfloat16
VMEM_BYTES = 56 * 1024 * 1024
GELU_A = 0.7978845608028654
GELU_B = 0.044715 * GELU_A
SWAP = [(0, 0), (1, 2), (2, 1), (3, 3)]


def dot(a, b, ca, cb):
    return lax.dot_general(a, b, (((ca,), (cb,)), ((), ())), preferred_element_type=F32)


def params(grid_dims=1):
    return pltpu.CompilerParams(
        vmem_limit_bytes=VMEM_BYTES, dimension_semantics=("arbitrary",) * grid_dims
    )


def cost(flops, nbytes, trans=0):
    return pl.CostEstimate(flops=int(flops), bytes_accessed=int(nbytes), transcendentals=int(trans))


def head_stack(block):
    lane = lax.broadcasted_iota(jnp.int32, block.shape, 1)
    zero = jnp.zeros_like(block)
    return jnp.concatenate(
        [jnp.where(lane < HDIM, block, zero), jnp.where(lane < HDIM, zero, block)], axis=0
    )


def head_merge(stacked):
    lane = lax.broadcasted_iota(jnp.int32, (QLEN, LANES), 1)
    return jnp.where(lane < HDIM, stacked[:QLEN], stacked[QLEN:])


def pair_views(own_ref, oth_ref, found_ref, question, pair, local_hd, width):
    ref = own_ref if pair * LANES < local_hd else oth_ref
    base = pair * LANES % local_hd
    rows = slice(question * QLEN, (question + 1) * QLEN)
    query = ref[rows, base : base + LANES]
    key = ref[rows, local_hd + base : local_hd + base + LANES]
    value = ref[rows, 2 * local_hd + base : 2 * local_hd + base + LANES]
    col = pair * LANES
    pref = [found_ref[question, :, c * width + col : c * width + col + LANES] for c in range(4)]
    keys = jnp.concatenate([key, pref[0], pref[1]], axis=0)
    values = jnp.concatenate([value, pref[2], pref[3]], axis=0)
    stack = head_stack(query * jnp.asarray(HDIM**-0.5, BF16))
    return stack, keys, values


def pair_probs(stack, keys, bias):
    logits = dot(keys, stack, 1, 1)
    logits = jnp.concatenate([logits[:QLEN], logits[QLEN:] + bias], axis=0)
    weights = jnp.exp(logits - jnp.max(logits, axis=0, keepdims=True))
    return weights * (1.0 / jnp.sum(weights, axis=0, keepdims=True))


def attention_kernel(own_ref, oth_ref, found_ref, bias_ref, mixed_ref, *, questions, local_hd, width):
    for question in range(questions):
        bias = bias_ref[question]
        for pair in range(width // LANES):
            stack, keys, values = pair_views(
                own_ref, oth_ref, found_ref, question, pair, local_hd, width
            )
            probs = pair_probs(stack, keys, bias).astype(BF16)
            mixed = head_merge(dot(probs, values, 0, 0)).astype(BF16)
            mixed_ref[question * QLEN : (question + 1) * QLEN, pair * LANES : (pair + 1) * LANES] = mixed


def attention(own, oth, found, bias, questions=2):
    rows, local_hd = own.shape[0], own.shape[1] // 3
    width = 2 * local_hd
    count = rows // QLEN
    slots = found.shape[1]
    block = questions * QLEN
    return pl.pallas_call(
        functools.partial(attention_kernel, questions=questions, local_hd=local_hd, width=width),
        grid=(count // questions,),
        in_specs=[
            pl.BlockSpec((block, 3 * local_hd), lambda i: (i, 0)),
            pl.BlockSpec((block, 3 * local_hd), lambda i: (i, 0)),
            pl.BlockSpec((questions, slots, 4 * width), lambda i: (i, 0, 0)),
            pl.BlockSpec((questions, 2 * slots, LANES), lambda i: (i, 0, 0)),
        ],
        out_specs=pl.BlockSpec((block, width), lambda i: (i, 0)),
        out_shape=jax.ShapeDtypeStruct((rows, width), BF16),
        compiler_params=params(),
        cost_estimate=cost(rows * width * 96 * 8, rows * width * 8, rows * 12 * 96),
        name="attend",
    )(own, oth, found, bias)


def attention_back_kernel(
    own_ref, oth_ref, found_ref, bias_ref, mixed_ref, down_ref, doth_ref, slot_ref, *, questions, local_hd, width
):
    for question in range(questions):
        bias = bias_ref[question]
        rows = slice(question * QLEN, (question + 1) * QLEN)
        total = None
        for pair in range(width // LANES):
            stack, keys, values = pair_views(
                own_ref, oth_ref, found_ref, question, pair, local_hd, width
            )
            probs = pair_probs(stack, keys, bias)
            grad_stack = head_stack(mixed_ref[rows, pair * LANES : (pair + 1) * LANES])
            prob_grad = dot(values, grad_stack, 1, 1)
            delta = jnp.sum(probs * prob_grad, axis=0, keepdims=True)
            logit_grad = probs * (prob_grad - delta)
            pref_part = logit_grad[QLEN:]
            total = pref_part if total is None else total + pref_part
            low = logit_grad.astype(BF16)
            scale = HDIM**-0.5
            query_grad = head_merge(dot(low, keys, 0, 0)) * scale
            key_grad = dot(low[:QLEN], stack, 1, 0)
            value_grad = dot(probs[:QLEN].astype(BF16), grad_stack, 1, 0)
            out = down_ref if pair * LANES < local_hd else doth_ref
            base = pair * LANES % local_hd
            out[rows, base : base + LANES] = query_grad.astype(BF16)
            out[rows, local_hd + base : local_hd + base + LANES] = key_grad.astype(BF16)
            out[rows, 2 * local_hd + base : 2 * local_hd + base + LANES] = value_grad.astype(BF16)
        slot_ref[question] = jnp.broadcast_to(jnp.sum(total, axis=1, keepdims=True), total.shape)


def attention_back(own, oth, found, bias, mixed_low, questions=2):
    rows, local_hd = own.shape[0], own.shape[1] // 3
    width = 2 * local_hd
    count = rows // QLEN
    slots = found.shape[1]
    block = questions * QLEN
    wide = pl.BlockSpec((block, 3 * local_hd), lambda i: (i, 0))
    bias_spec = pl.BlockSpec((questions, 2 * slots, LANES), lambda i: (i, 0, 0))
    return pl.pallas_call(
        functools.partial(
            attention_back_kernel, questions=questions, local_hd=local_hd, width=width
        ),
        grid=(count // questions,),
        in_specs=[
            wide,
            wide,
            pl.BlockSpec((questions, slots, 4 * width), lambda i: (i, 0, 0)),
            bias_spec,
            pl.BlockSpec((block, width), lambda i: (i, 0)),
        ],
        out_specs=[wide, wide, bias_spec],
        out_shape=[
            jax.ShapeDtypeStruct((rows, 3 * local_hd), BF16),
            jax.ShapeDtypeStruct((rows, 3 * local_hd), BF16),
            jax.ShapeDtypeStruct((count, 2 * slots, LANES), F32),
        ],
        compiler_params=params(),
        cost_estimate=cost(rows * width * 96 * 20, rows * width * 16, rows * 12 * 96),
        name="attend_back",
    )(own, oth, found, bias, mixed_low)


def rms_scale(block):
    return lax.rsqrt(jnp.mean(block * block, axis=-1, keepdims=True) + NORM_EPS)


def forward_kernel(
    x_ref, mixed_ref, out_own, out_oth, gain_ref, up_own, up_oth,
    resid_ref, normed_ref, hid_own, hid_oth, slope_own, slope_oth, presid_ref, phid_own, phid_oth, *, chunk
):
    rows = x_ref.shape[0]
    half = mixed_ref.shape[1] // 2
    residual = (
        x_ref[...].astype(F32)
        + dot(mixed_ref[:, :half], out_own[...], 1, 1)
        + dot(mixed_ref[:, half:], out_oth[...], 1, 1)
    )
    resid_ref[...] = residual
    presid_ref[...] = jnp.sum(residual.reshape(rows // RUN, RUN, residual.shape[1]), axis=1)
    normed = (residual * rms_scale(residual) * gain_ref[1:2]).astype(BF16)
    normed_ref[...] = normed
    run_of = lax.broadcasted_iota(jnp.int32, (rows // RUN, rows), 0)
    row_at = lax.broadcasted_iota(jnp.int32, (rows // RUN, rows), 1)
    low = run_of * RUN
    pool = jnp.where((row_at >= low) & (row_at < low + RUN), 1.0, 0.0).astype(BF16)
    for up_ref, hid_ref, slope_ref, phid_ref in (
        (up_own, hid_own, slope_own, phid_own),
        (up_oth, hid_oth, slope_oth, phid_oth),
    ):
        for at in range(0, up_ref.shape[1], chunk):
            cols = slice(at, at + chunk)
            pre = dot(normed, up_ref[:, cols], 1, 0)
            square = pre * pre
            cube = GELU_B * square
            bend = jnp.tanh(pre * (GELU_A + cube))
            half_pre = 0.5 * pre
            hidden = (half_pre * bend + half_pre).astype(BF16)
            hid_ref[:, cols] = hidden
            slope = (0.5 + 0.5 * bend) + half_pre * (1.0 - bend * bend) * (GELU_A + 3.0 * cube)
            slope_ref[:, cols] = slope.astype(BF16)
            phid_ref[:, cols] = dot(pool, hidden, 1, 0)


def forward(x, mixed, out_pair, gains, up_pair, tile=256, chunk=512):
    rows, width = x.shape
    local_ff = up_pair[0].shape[1]
    row = lambda cols: pl.BlockSpec((tile, cols), lambda i: (i, 0))
    pooled = lambda cols: pl.BlockSpec((tile // RUN, cols), lambda i: (i, 0))
    whole = lambda a: pl.BlockSpec(a.shape, lambda i: (0, 0))
    shape = jax.ShapeDtypeStruct
    return pl.pallas_call(
        functools.partial(forward_kernel, chunk=chunk),
        grid=(rows // tile,),
        in_specs=[row(width), row(width), whole(out_pair[0]), whole(out_pair[1]), whole(gains), whole(up_pair[0]), whole(up_pair[1])],
        out_specs=[row(width), row(width)] + [row(local_ff)] * 4 + [pooled(width), pooled(local_ff), pooled(local_ff)],
        out_shape=[
            shape((rows, width), F32),
            shape((rows, width), BF16),
            shape((rows, local_ff), BF16),
            shape((rows, local_ff), BF16),
            shape((rows, local_ff), BF16),
            shape((rows, local_ff), BF16),
            shape((rows // RUN, width), F32),
            shape((rows // RUN, local_ff), F32),
            shape((rows // RUN, local_ff), F32),
        ],
        compiler_params=params(),
        cost_estimate=cost(2 * rows * width * (width + 2 * local_ff), rows * (width * 9 + local_ff * 8) + width * (width + local_ff * 2) * 2, rows * local_ff * 2),
        name="out_up",
    )(x, mixed, *out_pair, gains, *up_pair)


def norm_back(block, grad, gain):
    scale = rms_scale(block)
    weighted = grad * gain
    inner = jnp.mean(block * weighted, axis=-1, keepdims=True)
    return (
        scale * weighted - block * (scale * scale * scale * inner),
        jnp.sum(grad * block * scale, axis=0, keepdims=True),
    )


def backward_kernel(
    cot_ref, spread_ref, resid_ref, slope_own, slope_oth, down_own, down_oth, up_own, up_oth, gain_ref, out_own, out_oth,
    result_ref, pre_own, pre_oth, rgrad_ref, attn_ref, mixed_ref, gain_grad_ref, *, chunk
):
    rows, width = cot_ref.shape
    spread = jnp.broadcast_to(spread_ref[...][:, None, :], (rows // RUN, RUN, width)).reshape(rows, width)
    result_grad = cot_ref[...].astype(F32) + spread
    result_low = result_grad.astype(BF16)
    result_ref[...] = result_low
    total = jnp.zeros((rows, width), F32)
    for down_ref, up_ref, slope_ref, pre_ref in (
        (down_own, up_own, slope_own, pre_own),
        (down_oth, up_oth, slope_oth, pre_oth),
    ):
        for at in range(0, up_ref.shape[1], chunk):
            cols = slice(at, at + chunk)
            hidden_grad = dot(result_low, down_ref[:, cols], 1, 0)
            pre_low = (hidden_grad * slope_ref[:, cols].astype(F32)).astype(BF16)
            pre_ref[:, cols] = pre_low
            total = total + dot(pre_low, up_ref[:, cols], 1, 1)
    part, gain_part = norm_back(resid_ref[...], total, gain_ref[1:2])
    residual_grad = result_grad + part
    rgrad_ref[...] = residual_grad
    attn_low = residual_grad.astype(BF16)
    attn_ref[...] = attn_low
    half = out_own.shape[1]
    mixed_ref[:, :half] = dot(attn_low, out_own[...], 1, 0).astype(BF16)
    mixed_ref[:, half:] = dot(attn_low, out_oth[...], 1, 0).astype(BF16)

    @pl.when(pl.program_id(0) == 0)
    def _():
        gain_grad_ref[...] = jnp.zeros_like(gain_grad_ref)

    gain_grad_ref[...] += jnp.broadcast_to(gain_part, gain_grad_ref.shape)


def backward(cot, spread, residual, slopes, down_pair, up_pair, gains, out_pair, tile=256, chunk=512):
    rows, width = cot.shape
    local_ff = up_pair[0].shape[1]
    row = lambda cols: pl.BlockSpec((tile, cols), lambda i: (i, 0))
    whole = lambda a: pl.BlockSpec(a.shape, lambda i: (0, 0))
    shape = jax.ShapeDtypeStruct
    return pl.pallas_call(
        functools.partial(backward_kernel, chunk=chunk),
        grid=(rows // tile,),
        in_specs=[
            row(width),
            pl.BlockSpec((tile // RUN, width), lambda i: (i, 0)),
            row(width),
            row(local_ff),
            row(local_ff),
            whole(down_pair[0]),
            whole(down_pair[1]),
            whole(up_pair[0]),
            whole(up_pair[1]),
            whole(gains),
            whole(out_pair[0]),
            whole(out_pair[1]),
        ],
        out_specs=[row(width), row(local_ff), row(local_ff), row(width), row(width), row(width), pl.BlockSpec((8, width), lambda i: (0, 0))],
        out_shape=[
            shape((rows, width), BF16),
            shape((rows, local_ff), BF16),
            shape((rows, local_ff), BF16),
            shape((rows, width), F32),
            shape((rows, width), BF16),
            shape((rows, width), BF16),
            shape((8, width), F32),
        ],
        compiler_params=params(),
        cost_estimate=cost(2 * rows * width * (width + 4 * local_ff), rows * (width * 16 + local_ff * 8) + width * (width + local_ff * 4) * 2),
        name="down_up_back",
    )(cot, spread, residual, *slopes, *down_pair, *up_pair, gains, *out_pair)


def input_kernel(x_ref, rgrad_ref, d_own, d_oth, w_own, w_oth, gain_ref, out_ref, gain_grad_ref):
    normed_grad = dot(d_own[...], w_own[...], 1, 1) + dot(d_oth[...], w_oth[...], 1, 1)
    part, gain_part = norm_back(x_ref[...].astype(F32), normed_grad, gain_ref[0:1])
    out_ref[...] = (rgrad_ref[...] + part).astype(BF16)

    @pl.when(pl.program_id(0) == 0)
    def _():
        gain_grad_ref[...] = jnp.zeros_like(gain_grad_ref)

    gain_grad_ref[...] += jnp.broadcast_to(gain_part, gain_grad_ref.shape)


def input_back(x, rgrad, d_pair, w_pair, gains, tile=256):
    rows, width = x.shape
    row = lambda cols: pl.BlockSpec((tile, cols), lambda i: (i, 0))
    whole = lambda a: pl.BlockSpec(a.shape, lambda i: (0, 0))
    wide = d_pair[0].shape[1]
    return pl.pallas_call(
        input_kernel,
        grid=(rows // tile,),
        in_specs=[row(width), row(width), row(wide), row(wide), whole(w_pair[0]), whole(w_pair[1]), whole(gains)],
        out_specs=[row(width), pl.BlockSpec((8, width), lambda i: (0, 0))],
        out_shape=[jax.ShapeDtypeStruct((rows, width), BF16), jax.ShapeDtypeStruct((8, width), F32)],
        compiler_params=params(),
        cost_estimate=cost(4 * rows * width * wide, rows * (width * 8 + wide * 4) + width * wide * 4),
        name="qkv_back",
    )(x, rgrad, *d_pair, *w_pair, gains)


def swapped(value):
    return lax.ppermute(value, ("half", "mp"), SWAP)


def from_mate(value):
    return lax.ppermute(value, "half", [(0, 1), (1, 0)])


def pick(value, index, axis=0):
    return lax.dynamic_index_in_dim(value, index, axis, keepdims=False)


def fetch(weight):
    own = swapped(weight)
    return own, from_mate(own)


def scatter_sum(own, oth):
    grad = (own.astype(F32) + from_mate(oth).astype(F32)).astype(BF16)
    shards = lax.axis_size("dp")
    if shards != 8:
        return lax.psum_scatter(grad.astype(F32), "dp", scatter_dimension=0, tiled=True)
    rows, cols = grad.shape
    index = lax.axis_index("dp")
    x_at, z_at = index % 2, index // 2
    view = grad.reshape(4, 2, rows // 8, cols)
    got = lax.ppermute(pick(view, 1 - x_at, 1), "dp", [(i, i ^ 1) for i in range(8)])
    part = (pick(view, x_at, 1).astype(F32) + got.astype(F32)).astype(BF16)
    up = down = None
    for step in range(1, 4):
        val = pick(part, jnp.minimum(z_at + 4 - step, 3))
        if up is not None:
            val = (val.astype(F32) + up.astype(F32)).astype(BF16)
        up = lax.ppermute(val, "dp", [(2 * z + x, 2 * z + 2 + x) for z in range(step) for x in range(2)])
        val = pick(part, jnp.maximum(z_at - 4 + step, 0))
        if down is not None:
            val = (val.astype(F32) + down.astype(F32)).astype(BF16)
        down = lax.ppermute(val, "dp", [(2 * z + x, 2 * z - 2 + x) for z in range(4 - step, 4) for x in range(2)])
    return pick(part, z_at).astype(F32) + up.astype(F32) + down.astype(F32)


def all_sum(value):
    return lax.psum(value, ("half", "dp"))


def body(tokens, norm_gains, qkv_w, out_w, up_w, down_w, memory, memory_ids, counts, prefix_mask, cotangent):
    core = lax.axis_index("half")
    layer = lax.axis_index("mp")
    shard_count = lax.axis_size("dp")
    shard_index = lax.axis_index("dp")
    rows, width = tokens.shape[1:]
    questions, k_most = memory_ids.shape
    mem_dev = memory.shape[1]
    score_scale = (4 * width) ** (-0.5)
    local_hd = qkv_w.shape[3]
    padded = 16

    qkv_pair = fetch(qkv_w[0].reshape(width, 3 * local_hd))
    x = swapped(tokens[0])
    gains = swapped(norm_gains[0])
    out_pair = fetch(out_w[0])
    up_pair = fetch(up_w[0])
    down_pair = fetch(down_w[0])
    cot = swapped(cotangent[0])

    slot_total = questions * k_most
    capacity = (slot_total + shard_count - 1) // shard_count
    table = memory[0].reshape(mem_dev, 4 * width)
    local_rows = jnp.concatenate(
        [memory_ids.reshape(-1) % mem_dev, jnp.zeros((capacity * shard_count - slot_total,), jnp.int32)]
    )
    requests = jnp.roll(local_rows.reshape(capacity, shard_count), shard_index, axis=1).T
    asked = lax.all_to_all(requests, "dp", split_axis=0, concat_axis=0, tiled=True).reshape(-1)
    answer = dot((asked[:, None] == jnp.arange(mem_dev)[None, :]).astype(BF16), table, 1, 0).astype(BF16)
    answers = lax.all_to_all(answer, "dp", split_axis=0, concat_axis=0, tiled=True)
    answers = swapped(answers)
    at = jnp.arange(questions * padded)
    slot = at % padded
    flat = at // padded * k_most + slot
    source = (shard_index + flat % shard_count) % shard_count * capacity + flat // shard_count
    source = jnp.where(slot < k_most, source, -1)
    chosen = (source[:, None] == jnp.arange(capacity * shard_count)[None, :]).astype(BF16)
    found = dot(chosen, answers, 1, 0).astype(BF16).reshape(questions, padded, 4 * width)
    halves = found.reshape(questions, padded, 4, 2, width // 2)
    found_heads = jnp.where(core == 0, found, halves[:, :, :, ::-1].reshape(found.shape))

    valid = (jnp.arange(k_most)[None, :] < counts[:, None])[:, None, :] & (
        jnp.swapaxes(prefix_mask.reshape(questions, k_most, 2), 1, 2) == 1
    )
    valid = jnp.pad(valid.astype(F32), ((0, 0), (0, 0), (0, padded - k_most))).reshape(questions, 2 * padded)
    valid = (swapped(valid) > 0.5) & (layer == 1)

    def biases(scores):
        wide = jnp.tile(jnp.pad(scores.astype(F32), ((0, 0), (0, padded - k_most))), (1, 2))
        bias = jnp.where(valid, wide, MASKED)
        return jnp.broadcast_to(bias[:, :, None], (questions, 2 * padded, LANES))

    x32 = x.astype(F32)
    normed = (x32 * rms_scale(x32) * gains[0]).astype(BF16)
    proj = tuple(dot(normed, w, 1, 0).astype(BF16) for w in qkv_pair)

    def layer_forward(scores):
        bias = biases(scores)
        mixed = attention(*proj, found_heads, bias)
        return bias, mixed, forward(x, mixed, out_pair, gains, up_pair)

    first = layer_forward(jnp.zeros((questions, k_most), BF16))[2]
    pooled = first[6] + sum(
        lax.dot_general(p, w.astype(F32), (((1,), (1,)), ((), ())), precision=HIGHEST, preferred_element_type=F32)
        for p, w in zip(first[7:9], down_pair)
    )
    pooled = (pooled * (1.0 / RUN)).reshape(questions, 4 * width)
    scores = jnp.sum(pooled[:, None, :] * found[:, :k_most].astype(F32), axis=-1) * score_scale
    sent = lax.ppermute(scores.astype(BF16), "mp", [(0, 1)])

    bias, mixed, (residual, normed_two, hid_own, hid_oth, slope_own, slope_oth, _, _, _) = layer_forward(sent)

    def layer_backward(spread):
        result_low, pre_own, pre_oth, rgrad, attn_low, mixed_low, gain_two = backward(
            cot, spread, residual, (slope_own, slope_oth), down_pair, up_pair, gains, out_pair
        )
        d_own, d_oth, slot_grad = attention_back(*proj, found_heads, bias, mixed_low)
        return result_low, (pre_own, pre_oth), rgrad, attn_low, gain_two, (d_own, d_oth), slot_grad

    slot_grad = layer_backward(jnp.zeros((rows // RUN, width), F32))[-1][:, :, 0]
    score_low = (slot_grad[:, :k_most] + slot_grad[:, padded : padded + k_most]).astype(BF16)
    score_in = lax.ppermute(score_low, "mp", [(1, 0)])
    scale = score_scale / RUN
    spread = jnp.sum(
        (score_in.astype(F32) * scale)[:, :, None] * found[:, :k_most].astype(F32), axis=1
    ).reshape(rows // RUN, width)
    result_low, pre_pair, rgrad, attn_low, gain_two, d_pair, _ = layer_backward(spread)
    grad_in, gain_one = input_back(x, rgrad, d_pair, qkv_pair, gains)

    result = residual + dot(hid_own, down_pair[0], 1, 1) + dot(hid_oth, down_pair[1], 1, 1)
    activations = swapped(result.astype(BF16))
    input_grad = swapped(grad_in).astype(F32)
    score_out = swapped(jnp.where(layer == 1, score_low, score_in)).astype(F32)
    gain_grads = swapped(all_sum(jnp.concatenate([gain_one[:1], gain_two[:1]], axis=0)))

    def weight_grad(rows_of, cols_of):
        return dot(rows_of, cols_of, 0, 0).astype(BF16)

    local_mixed = (mixed[:, :local_hd], mixed[:, local_hd:])
    down_g = swapped(scatter_sum(weight_grad(result_low, hid_own), weight_grad(result_low, hid_oth)))
    up_g = swapped(scatter_sum(*(weight_grad(normed_two, p) for p in pre_pair)))
    out_g = swapped(scatter_sum(*(weight_grad(attn_low, m) for m in local_mixed)))
    qkv_g = swapped(scatter_sum(*(weight_grad(normed, d) for d in d_pair)))
    return (
        activations[None],
        input_grad[None],
        score_out,
        gain_grads[None],
        qkv_g.reshape(1, -1, 3, local_hd),
        out_g[None],
        up_g[None],
        down_g[None],
    )


def solution(mesh):
    placed = (
        P("half", ("dp", "mp"), None),
        P("half", None, None),
        P("half", None, None, "mp"),
        P("half", None, "mp"),
        P("half", None, "mp"),
        P("half", None, "mp"),
        P("half", "dp", None, None),
        P(("dp", "mp"), None),
        P(("dp", "mp")),
        P(("dp", "mp"), None),
        P("half", ("dp", "mp"), None),
    )
    return jax.shard_map(
        body,
        mesh=mesh,
        in_specs=placed,
        out_specs=(
            P("half", ("dp", "mp"), None),
            P("half", ("dp", "mp"), None),
            P(("dp", "mp"), None),
            P("half", None, None),
            P("half", "dp", None, "mp"),
            P("half", "dp", "mp"),
            P("half", "dp", "mp"),
            P("half", "dp", "mp"),
        ),
        check_vma=False,
    )
```

```python
import functools

import jax
import jax.numpy as jnp
from jax import lax
from jax.experimental import pallas as pl
from jax.experimental.pallas import tpu as pltpu
from jax.sharding import PartitionSpec as P

HDIM = 64
QLEN = 64
RUN = 16
LANES = 128
NORM_EPS = 1e-06
MASKED = -1e30
F32 = jnp.float32
BF16 = jnp.bfloat16
GELU_A = 0.7978845608028654
GELU_B = 0.044715 * GELU_A


def dot(a, b, ca, cb):
    return lax.dot_general(a, b, (((ca,), (cb,)), ((), ())), preferred_element_type=F32)


def params(mebibytes):
    return pltpu.CompilerParams(vmem_limit_bytes=mebibytes << 20)


def cost(flops, nbytes, trans=0):
    return pl.CostEstimate(flops=int(flops), bytes_accessed=int(nbytes), transcendentals=int(trans))


def head_stack(block):
    lane = lax.broadcasted_iota(jnp.int32, block.shape, 1)
    zero = jnp.zeros_like(block)
    return jnp.concatenate(
        [jnp.where(lane < HDIM, block, zero), jnp.where(lane < HDIM, zero, block)], axis=0
    )


def head_merge(stacked):
    lane = lax.broadcasted_iota(jnp.int32, (QLEN, LANES), 1)
    return jnp.where(lane < HDIM, stacked[:QLEN], stacked[QLEN:])


def pair_views(own_ref, oth_ref, found_ref, question, pair, local_hd, width):
    ref = own_ref if pair * LANES < local_hd else oth_ref
    base = pair * LANES % local_hd
    rows = slice(question * QLEN, (question + 1) * QLEN)
    query = ref[rows, base : base + LANES]
    key = ref[rows, local_hd + base : local_hd + base + LANES]
    value = ref[rows, 2 * local_hd + base : 2 * local_hd + base + LANES]
    stack = head_stack(query * jnp.asarray(HDIM**-0.5, BF16))
    if found_ref is None:
        return stack, key, value
    col = pair * LANES
    pref = [found_ref[question, :, c * width + col : c * width + col + LANES] for c in range(4)]
    keys = jnp.concatenate([key, pref[0], pref[1]], axis=0)
    values = jnp.concatenate([value, pref[2], pref[3]], axis=0)
    return stack, keys, values


def pair_logits(stack, keys, bias):
    logits = dot(keys, stack, 1, 1)
    if bias is None:
        return logits
    return jnp.concatenate([logits[:QLEN], logits[QLEN:] + bias], axis=0)


def softmax_down(logits):
    weights = jnp.exp(logits - jnp.max(logits, axis=0, keepdims=True))
    return weights * (1.0 / jnp.sum(weights, axis=0, keepdims=True))


def grouped(questions, pairs, group):
    items = [(question, pair) for question in range(questions) for pair in range(pairs)]
    return [items[at : at + group] for at in range(0, len(items), group)]


def attention_kernel(own_ref, oth_ref, *refs, questions, local_hd, width, group):
    found_ref, bias_ref, mixed_ref = refs if len(refs) == 3 else (None, None, *refs)
    for items in grouped(questions, width // LANES, group):
        views = [pair_views(own_ref, oth_ref, found_ref, q, p, local_hd, width) for q, p in items]
        logits = [pair_logits(v[0], v[1], None if bias_ref is None else bias_ref[q]) for v, (q, p) in zip(views, items)]
        probs = [softmax_down(l).astype(BF16) for l in logits]
        mixed = [dot(p, v[2], 0, 0) for p, v in zip(probs, views)]
        for m, (q, p) in zip(mixed, items):
            mixed_ref[q * QLEN : (q + 1) * QLEN, p * LANES : (p + 1) * LANES] = head_merge(m).astype(BF16)


def attention(own, oth, prefix=(), questions=4, group=12):
    rows, local_hd = own.shape[0], own.shape[1] // 3
    width = 2 * local_hd
    count = rows // QLEN
    block = questions * QLEN
    return pl.pallas_call(
        functools.partial(attention_kernel, questions=questions, local_hd=local_hd, width=width, group=group),
        grid=(count // questions,),
        in_specs=[pl.BlockSpec((block, 3 * local_hd), lambda i: (i, 0))] * 2
        + [pl.BlockSpec((questions, *a.shape[1:]), lambda i: (i, 0, 0)) for a in prefix],
        out_specs=pl.BlockSpec((block, width), lambda i: (i, 0)),
        out_shape=jax.ShapeDtypeStruct((rows, width), BF16),
        compiler_params=params(20),
        cost_estimate=cost(rows * width * 96 * 8, rows * width * 8, rows * 12 * 96),
        name="attend",
    )(own, oth, *prefix)


def attention_back_kernel(
    own_ref, oth_ref, found_ref, bias_ref, mixed_ref, down_ref, doth_ref, slot_ref, *, questions, local_hd, width, group
):
    totals = [None] * questions
    for items in grouped(questions, width // LANES, group):
        views = [pair_views(own_ref, oth_ref, found_ref, q, p, local_hd, width) for q, p in items]
        logits = [pair_logits(v[0], v[1], bias_ref[q]) for v, (q, p) in zip(views, items)]
        grads = [
            head_stack(mixed_ref[q * QLEN : (q + 1) * QLEN, p * LANES : (p + 1) * LANES]) for q, p in items
        ]
        prob_grads = [dot(v[2], g, 1, 1) for v, g in zip(views, grads)]
        probs = [softmax_down(l) for l in logits]
        deltas = [jnp.sum(p * g, axis=0, keepdims=True) for p, g in zip(probs, prob_grads)]
        logit_grads = [p * (g - d) for p, g, d in zip(probs, prob_grads, deltas)]
        lows = [l.astype(BF16) for l in logit_grads]
        value_grads = [dot(p[:QLEN].astype(BF16), g, 1, 0) for p, g in zip(probs, grads)]
        key_grads = [dot(l[:QLEN], v[0], 1, 0) for l, v in zip(lows, views)]
        query_grads = [dot(l, v[1], 0, 0) for l, v in zip(lows, views)]
        for at, (q, p) in enumerate(items):
            part = logit_grads[at][QLEN:]
            totals[q] = part if totals[q] is None else totals[q] + part
            out = down_ref if p * LANES < local_hd else doth_ref
            base = p * LANES % local_hd
            rows = slice(q * QLEN, (q + 1) * QLEN)
            out[rows, base : base + LANES] = (head_merge(query_grads[at]) * HDIM**-0.5).astype(BF16)
            out[rows, local_hd + base : local_hd + base + LANES] = key_grads[at].astype(BF16)
            out[rows, 2 * local_hd + base : 2 * local_hd + base + LANES] = value_grads[at].astype(BF16)
    for q in range(questions):
        slot_ref[q] = jnp.broadcast_to(jnp.sum(totals[q], axis=1, keepdims=True), totals[q].shape)


def attention_back(own, oth, found, bias, mixed_low, questions=2, group=12):
    rows, local_hd = own.shape[0], own.shape[1] // 3
    width = 2 * local_hd
    count = rows // QLEN
    slots = found.shape[1]
    block = questions * QLEN
    wide = pl.BlockSpec((block, 3 * local_hd), lambda i: (i, 0))
    bias_spec = pl.BlockSpec((questions, 2 * slots, LANES), lambda i: (i, 0, 0))
    return pl.pallas_call(
        functools.partial(
            attention_back_kernel, questions=questions, local_hd=local_hd, width=width, group=group
        ),
        grid=(count // questions,),
        in_specs=[
            wide,
            wide,
            pl.BlockSpec((questions, slots, 4 * width), lambda i: (i, 0, 0)),
            bias_spec,
            pl.BlockSpec((block, width), lambda i: (i, 0)),
        ],
        out_specs=[wide, wide, bias_spec],
        out_shape=[
            jax.ShapeDtypeStruct((rows, 3 * local_hd), BF16),
            jax.ShapeDtypeStruct((rows, 3 * local_hd), BF16),
            jax.ShapeDtypeStruct((count, 2 * slots, LANES), F32),
        ],
        compiler_params=params(24),
        cost_estimate=cost(rows * width * 96 * 20, rows * width * 16, rows * 12 * 96),
        name="attend_back",
    )(own, oth, found, bias, mixed_low)


def slot_kernel(own_ref, oth_ref, found_ref, bias_ref, mixed_ref, slot_ref, *, questions, local_hd, width, group):
    totals = [None] * questions
    for items in grouped(questions, width // LANES, group):
        views = [pair_views(own_ref, oth_ref, found_ref, q, p, local_hd, width) for q, p in items]
        logits = [pair_logits(v[0], v[1], bias_ref[q]) for v, (q, p) in zip(views, items)]
        grads = [
            head_stack(mixed_ref[q * QLEN : (q + 1) * QLEN, p * LANES : (p + 1) * LANES]) for q, p in items
        ]
        prob_grads = [dot(v[2], g, 1, 1) for v, g in zip(views, grads)]
        probs = [softmax_down(l) for l in logits]
        deltas = [jnp.sum(p * g, axis=0, keepdims=True) for p, g in zip(probs, prob_grads)]
        parts = [p[QLEN:] * (g[QLEN:] - d) for p, g, d in zip(probs, prob_grads, deltas)]
        for part, (q, p) in zip(parts, items):
            totals[q] = part if totals[q] is None else totals[q] + part
    for q in range(questions):
        slot_ref[q] = jnp.broadcast_to(jnp.sum(totals[q], axis=1, keepdims=True), totals[q].shape)


def slot_sums(own, oth, found, bias, mixed_low, questions=4, group=12):
    rows, local_hd = own.shape[0], own.shape[1] // 3
    width = 2 * local_hd
    count = rows // QLEN
    slots = found.shape[1]
    block = questions * QLEN
    wide = pl.BlockSpec((block, 3 * local_hd), lambda i: (i, 0))
    bias_spec = pl.BlockSpec((questions, 2 * slots, LANES), lambda i: (i, 0, 0))
    return pl.pallas_call(
        functools.partial(slot_kernel, questions=questions, local_hd=local_hd, width=width, group=group),
        grid=(count // questions,),
        in_specs=[
            wide,
            wide,
            pl.BlockSpec((questions, slots, 4 * width), lambda i: (i, 0, 0)),
            bias_spec,
            pl.BlockSpec((block, width), lambda i: (i, 0)),
        ],
        out_specs=bias_spec,
        out_shape=jax.ShapeDtypeStruct((count, 2 * slots, LANES), F32),
        compiler_params=params(20),
        cost_estimate=cost(rows * width * 96 * 8, rows * width * 12, rows * 12 * 96),
        name="slot_sums",
    )(own, oth, found, bias, mixed_low)


def rms_scale(block):
    return lax.rsqrt(jnp.mean(block * block, axis=-1, keepdims=True) + NORM_EPS)


def row_tiles(rows, tile):
    return [slice(at, at + tile) for at in range(0, rows, tile)]


def whole(array):
    return pl.BlockSpec(array.shape, lambda i: (0,) * array.ndim)


def whole_shape(shape):
    return pl.BlockSpec(shape, lambda i: (0, 0))


def first_cols(rows, chunk, steps):
    return pl.BlockSpec((rows, chunk), lambda i: (0, jnp.minimum(i, steps - 1)))


def second_cols(rows, chunk, steps):
    return pl.BlockSpec((rows, chunk), lambda i: (0, jnp.maximum(i - steps, 0)))


def by_half(steps, first, second):
    index = pl.program_id(0)
    pl.when(index < steps)(first)
    pl.when(index >= steps)(second)


def project_kernel(x_ref, gain_ref, w_own, w_oth, normed_ref, own_ref, oth_ref, *, tile, steps):
    tiles = row_tiles(x_ref.shape[0], tile)

    @pl.when(pl.program_id(0) == 0)
    def _():
        for at in tiles:
            block = x_ref[at].astype(F32)
            normed_ref[at] = (block * rms_scale(block) * gain_ref[0:1]).astype(BF16)

    def run(w_ref, out_ref):
        for at in tiles:
            out_ref[at] = dot(normed_ref[at], w_ref[...], 1, 0).astype(BF16)

    by_half(steps, lambda: run(w_own, own_ref), lambda: run(w_oth, oth_ref))


def project(x, gains, w_pair, tile=256, chunk=384):
    rows, width = x.shape
    cols = w_pair[0].shape[1]
    steps = cols // chunk
    shape = jax.ShapeDtypeStruct
    return pl.pallas_call(
        functools.partial(project_kernel, tile=tile, steps=steps),
        grid=(2 * steps,),
        in_specs=[whole(x), whole(gains), first_cols(width, chunk, steps), second_cols(width, chunk, steps)],
        out_specs=[whole(x), first_cols(rows, chunk, steps), second_cols(rows, chunk, steps)],
        out_shape=[shape((rows, width), BF16), shape((rows, cols), BF16), shape((rows, cols), BF16)],
        compiler_params=params(24),
        cost_estimate=cost(4 * rows * width * cols, rows * (width + cols) * 4 + width * cols * 4),
        name="project",
    )(x, gains, *w_pair)


def norm_back(block, grad, gain):
    scale = rms_scale(block)
    weighted = grad * gain
    inner = jnp.mean(block * weighted, axis=-1, keepdims=True)
    return (
        scale * weighted - block * (scale * scale * scale * inner),
        jnp.sum(grad * block * scale, axis=0, keepdims=True),
    )


def gelu_terms(pre):
    cube = GELU_B * (pre * pre)
    return cube, jnp.tanh(pre * (GELU_A + cube)), 0.5 * pre


def gelu_value(terms):
    _, bend, half_pre = terms
    return half_pre * bend + half_pre


def gelu_slope(terms):
    cube, bend, half_pre = terms
    return (0.5 + 0.5 * bend) + half_pre * (1.0 - bend * bend) * (GELU_A + 3.0 * cube)


def residual_rows(at, x_ref, mixed_ref, out_own, out_oth):
    half = mixed_ref.shape[1] // 2
    return (
        x_ref[at].astype(F32)
        + dot(mixed_ref[at, :half], out_own[...], 1, 1)
        + dot(mixed_ref[at, half:], out_oth[...], 1, 1)
    )


def normed_rows(residual, gain):
    return (residual * rms_scale(residual) * gain).astype(BF16)


def score_kernel(
    x_ref, mixed_ref, out_own, out_oth, gain_ref, up_own, up_oth, down_own, down_oth,
    pooled_ref, normed_ref, total_ref, *, tile, steps
):
    index = pl.program_id(0)
    tiles = row_tiles(x_ref.shape[0], tile)

    @pl.when(index == 0)
    def _():
        for at in tiles:
            residual = residual_rows(at, x_ref, mixed_ref, out_own, out_oth)
            total_ref[at] = residual
            normed_ref[at] = normed_rows(residual, gain_ref[1:2])

    def run(up_ref, down_ref):
        for at in tiles:
            hidden = gelu_value(gelu_terms(dot(normed_ref[at], up_ref[...], 1, 0))).astype(BF16)
            total_ref[at] += dot(hidden, down_ref[...], 1, 1)

    by_half(steps, lambda: run(up_own, down_own), lambda: run(up_oth, down_oth))

    @pl.when(index == 2 * steps - 1)
    def _():
        for at in tiles:
            result = total_ref[at]
            runs = slice(at.start // RUN, at.stop // RUN)
            pooled_ref[runs] = jnp.sum(result.reshape(tile // RUN, RUN, result.shape[1]), axis=1)


def once(array):
    return pl.BlockSpec(array.shape, lambda i: (0,) * array.ndim, pipeline_mode=pl.Buffered(1))


def pooled_result(x, mixed, out_pair, gains, up_pair, down_pair, tile=256, chunk=768):
    rows, width = x.shape
    local_ff = up_pair[0].shape[1]
    steps = local_ff // chunk
    cols = [first_cols(width, chunk, steps), second_cols(width, chunk, steps)]
    return pl.pallas_call(
        functools.partial(score_kernel, tile=tile, steps=steps),
        grid=(2 * steps,),
        in_specs=[once(x), once(mixed), once(out_pair[0]), once(out_pair[1]), once(gains)] + cols * 2,
        out_specs=whole_shape((rows // RUN, width)),
        out_shape=jax.ShapeDtypeStruct((rows // RUN, width), F32),
        scratch_shapes=[pltpu.VMEM((rows, width), BF16), pltpu.VMEM((rows, width), F32)],
        compiler_params=params(30),
        cost_estimate=cost(2 * rows * width * (width + 4 * local_ff), rows * width * 4 + width * (width + local_ff * 4) * 2, rows * local_ff * 2),
        name="pooled_result",
    )(x, mixed, *out_pair, gains, *up_pair, *down_pair)


def early_kernel(
    x_ref, mixed_ref, cot_ref, out_own, out_oth, gain_ref, up_own, up_oth, down_own, down_oth,
    result_ref, slope_own, slope_oth, grad_own, grad_oth, run_own, run_oth,
    normed_ref, sum_ref, left_ref, hid_ref, *, tile, steps
):
    index = pl.program_id(0)
    rows, width = x_ref.shape
    runs = rows // RUN
    tiles = row_tiles(rows, tile)

    @pl.when(index == 0)
    def _():
        for at in tiles:
            residual = residual_rows(at, x_ref, mixed_ref, out_own, out_oth)
            sum_ref[at] = residual
            normed_ref[at] = normed_rows(residual, gain_ref[1:2])
            left_ref[:width, at] = cot_ref[at].T
        run_of = lax.broadcasted_iota(jnp.int32, (runs, rows), 0) * RUN
        row_at = lax.broadcasted_iota(jnp.int32, (runs, rows), 1)
        left_ref[width:] = jnp.where((row_at >= run_of) & (row_at < run_of + RUN), 1.0, 0.0).astype(BF16)

    def run(up_ref, down_ref, slope_ref, grad_ref, run_ref):
        for at in tiles:
            terms = gelu_terms(dot(normed_ref[at], up_ref[...], 1, 0))
            hidden = gelu_value(terms).astype(BF16)
            hid_ref[at] = hidden
            slope_ref[at] = gelu_slope(terms).astype(BF16)
            sum_ref[at] += dot(hidden, down_ref[...], 1, 1)
        for at in row_tiles(width, tile):
            grad_ref[at] = dot(left_ref[at], hid_ref[...], 1, 0).astype(BF16)
        run_ref[...] = dot(left_ref[width:], hid_ref[...], 1, 0).astype(BF16)

    by_half(
        steps,
        lambda: run(up_own, down_own, slope_own, grad_own, run_own),
        lambda: run(up_oth, down_oth, slope_oth, grad_oth, run_oth),
    )

    @pl.when(index == 2 * steps - 1)
    def _():
        for at in tiles:
            result_ref[at] = sum_ref[at].astype(BF16)


def early_part(x, mixed, cot, out_pair, gains, up_pair, down_pair, tile=256, chunk=512):
    rows, width = x.shape
    local_ff = up_pair[0].shape[1]
    runs = rows // RUN
    steps = local_ff // chunk
    shape = jax.ShapeDtypeStruct
    cols = lambda height: [first_cols(height, chunk, steps), second_cols(height, chunk, steps)]
    return pl.pallas_call(
        functools.partial(early_kernel, tile=tile, steps=steps),
        grid=(2 * steps,),
        in_specs=[once(x), once(mixed), once(cot), once(out_pair[0]), once(out_pair[1]), once(gains)] + cols(width) * 2,
        out_specs=[once(x)] + cols(rows) + cols(width) + cols(runs),
        out_shape=[shape((rows, width), BF16)]
        + [shape((rows, local_ff), BF16)] * 2
        + [shape((width, local_ff), BF16)] * 2
        + [shape((runs, local_ff), BF16)] * 2,
        scratch_shapes=[
            pltpu.VMEM((rows, width), BF16),
            pltpu.VMEM((rows, width), F32),
            pltpu.VMEM((width + runs, rows), BF16),
            pltpu.VMEM((rows, chunk), BF16),
        ],
        compiler_params=params(40),
        cost_estimate=cost(2 * rows * width * (width + 6 * local_ff), rows * (width * 8 + local_ff * 4) + width * (width + local_ff * 6) * 2, rows * local_ff * 2),
        name="early_part",
    )(x, mixed, cot, *out_pair, gains, *up_pair, *down_pair)


def finish_rows(tiles, grad_of, resid_ref, total_ref, gain_ref, out_own, out_oth, attn_ref, mgrad_ref, gain_grad_ref):
    half = out_own.shape[1]
    gain_total = jnp.zeros((1, resid_ref.shape[1]), F32)
    for at in tiles:
        part, gain_part = norm_back(resid_ref[at], total_ref[at], gain_ref[1:2])
        gain_total = gain_total + gain_part
        attn_low = (grad_of(at) + part).astype(BF16)
        attn_ref[at] = attn_low
        mgrad_ref[at, :half] = dot(attn_low, out_own[...], 1, 0).astype(BF16)
        mgrad_ref[at, half:] = dot(attn_low, out_oth[...], 1, 0).astype(BF16)
    gain_grad_ref[...] = jnp.broadcast_to(gain_total, gain_grad_ref.shape)


def join_kernel(
    x_ref, mixed_ref, cot_ref, out_own, out_oth, gain_ref, up_own, up_oth, down_own, down_oth,
    attn_ref, mgrad_ref, gain_grad_ref, hid_own, hid_oth, pre_own, pre_oth,
    normed_ref, resid_ref, total_ref, *, tile, steps
):
    index = pl.program_id(0)
    tiles = row_tiles(x_ref.shape[0], tile)

    @pl.when(index == 0)
    def _():
        total_ref[...] = jnp.zeros_like(total_ref)
        for at in tiles:
            residual = residual_rows(at, x_ref, mixed_ref, out_own, out_oth)
            resid_ref[at] = residual
            normed_ref[at] = normed_rows(residual, gain_ref[1:2])

    def run(up_ref, down_ref, hid_ref, pre_ref):
        for at in tiles:
            terms = gelu_terms(dot(normed_ref[at], up_ref[...], 1, 0))
            hid_ref[at] = gelu_value(terms).astype(BF16)
            pre_low = (dot(cot_ref[at], down_ref[...], 1, 0) * gelu_slope(terms)).astype(BF16)
            pre_ref[at] = pre_low
            total_ref[at] += dot(pre_low, up_ref[...], 1, 1)

    by_half(
        steps,
        lambda: run(up_own, down_own, hid_own, pre_own),
        lambda: run(up_oth, down_oth, hid_oth, pre_oth),
    )

    @pl.when(index == 2 * steps - 1)
    def _():
        finish_rows(
            tiles, lambda at: cot_ref[at].astype(F32), resid_ref, total_ref, gain_ref, out_own, out_oth, attn_ref, mgrad_ref, gain_grad_ref
        )


def join_part(x, mixed, cot, out_pair, gains, up_pair, down_pair, tile=256, chunk=768):
    rows, width = x.shape
    local_ff = up_pair[0].shape[1]
    steps = local_ff // chunk
    shape = jax.ShapeDtypeStruct
    cols = lambda height: [first_cols(height, chunk, steps), second_cols(height, chunk, steps)]
    return pl.pallas_call(
        functools.partial(join_kernel, tile=tile, steps=steps),
        grid=(2 * steps,),
        in_specs=[once(x), once(mixed), once(cot), once(out_pair[0]), once(out_pair[1]), once(gains)] + cols(width) * 2,
        out_specs=[once(x), once(x), whole_shape((8, width))] + cols(rows) * 2,
        out_shape=[shape((rows, width), BF16)] * 2 + [shape((8, width), F32)] + [shape((rows, local_ff), BF16)] * 4,
        scratch_shapes=[
            pltpu.VMEM((rows, width), BF16),
            pltpu.VMEM((rows, width), F32),
            pltpu.VMEM((rows, width), F32),
        ],
        compiler_params=params(48),
        cost_estimate=cost(4 * rows * width * (width + 3 * local_ff), rows * (width * 10 + local_ff * 8) + width * (width + local_ff * 4) * 2, rows * local_ff * 2),
        name="join_part",
    )(x, mixed, cot, *out_pair, gains, *up_pair, *down_pair)


def join_grads_kernel(
    x_ref, mixed_ref, out_own, out_oth, gain_ref, down_own, down_oth, hid_own, hid_oth, pre_own, pre_oth,
    result_ref, up_g_own, up_g_oth, normed_t, sum_ref, *, tile, steps
):
    index = pl.program_id(0)
    width = x_ref.shape[1]
    tiles = row_tiles(x_ref.shape[0], tile)

    @pl.when(index == 0)
    def _():
        for at in tiles:
            residual = residual_rows(at, x_ref, mixed_ref, out_own, out_oth)
            sum_ref[at] = residual
            normed_t[:, at] = normed_rows(residual, gain_ref[1:2]).T

    def run(down_ref, hid_ref, pre_ref, up_g):
        for at in row_tiles(width, tile):
            up_g[at] = dot(normed_t[at], pre_ref[...], 1, 0).astype(BF16)
        for at in tiles:
            sum_ref[at] += dot(hid_ref[at], down_ref[...], 1, 1)

    by_half(
        steps,
        lambda: run(down_own, hid_own, pre_own, up_g_own),
        lambda: run(down_oth, hid_oth, pre_oth, up_g_oth),
    )

    @pl.when(index == 2 * steps - 1)
    def _():
        for at in tiles:
            result_ref[at] = sum_ref[at].astype(BF16)


def join_grads(x, mixed, out_pair, gains, down_pair, hid_pair, pre_pair, tile=256, chunk=512):
    rows, width = x.shape
    local_ff = down_pair[0].shape[1]
    steps = local_ff // chunk
    shape = jax.ShapeDtypeStruct
    cols = lambda height: [first_cols(height, chunk, steps), second_cols(height, chunk, steps)]
    return pl.pallas_call(
        functools.partial(join_grads_kernel, tile=tile, steps=steps),
        grid=(2 * steps,),
        in_specs=[once(x), once(mixed), once(out_pair[0]), once(out_pair[1]), once(gains)] + cols(width) + cols(rows) * 2,
        out_specs=[once(x)] + cols(width),
        out_shape=[shape((rows, width), BF16)] + [shape((width, local_ff), BF16)] * 2,
        scratch_shapes=[
            pltpu.VMEM((width, rows), BF16),
            pltpu.VMEM((rows, width), F32),
        ],
        compiler_params=params(40),
        cost_estimate=cost(2 * rows * width * (width + 6 * local_ff), rows * (width * 8 + local_ff * 8) + width * (width + local_ff * 6) * 2),
        name="join_grads",
    )(x, mixed, *out_pair, gains, *down_pair, *hid_pair, *pre_pair)


def late_kernel(
    x_ref, mixed_ref, cot_ref, spread_ref, out_own, out_oth, gain_ref, up_own, up_oth, down_own, down_oth, slope_own, slope_oth,
    attn_ref, mgrad_ref, gain_grad_ref, up_g_own, up_g_oth,
    normed_t, grad_ref, resid_ref, total_ref, pre_ref, *, tile, steps
):
    index = pl.program_id(0)
    width = x_ref.shape[1]
    tiles = row_tiles(x_ref.shape[0], tile)

    def result_grad(at):
        runs = slice(at.start // RUN, at.stop // RUN)
        spread = jnp.broadcast_to(spread_ref[runs][:, None, :], (tile // RUN, RUN, width)).reshape(tile, width)
        return cot_ref[at].astype(F32) + spread

    @pl.when(index == 0)
    def _():
        total_ref[...] = jnp.zeros_like(total_ref)
        for at in tiles:
            residual = residual_rows(at, x_ref, mixed_ref, out_own, out_oth)
            resid_ref[at] = residual
            normed_t[:, at] = normed_rows(residual, gain_ref[1:2]).T
            grad_ref[at] = result_grad(at).astype(BF16)

    def run(up_ref, down_ref, slope_ref, up_g):
        for at in tiles:
            pre_low = (dot(grad_ref[at], down_ref[...], 1, 0) * slope_ref[at].astype(F32)).astype(BF16)
            pre_ref[at] = pre_low
            total_ref[at] += dot(pre_low, up_ref[...], 1, 1)
        for at in row_tiles(width, tile):
            up_g[at] = dot(normed_t[at], pre_ref[...], 1, 0).astype(BF16)

    by_half(
        steps,
        lambda: run(up_own, down_own, slope_own, up_g_own),
        lambda: run(up_oth, down_oth, slope_oth, up_g_oth),
    )

    @pl.when(index == 2 * steps - 1)
    def _():
        finish_rows(
            tiles, result_grad, resid_ref, total_ref, gain_ref, out_own, out_oth, attn_ref, mgrad_ref, gain_grad_ref
        )


def late_part(x, mixed, cot, spread, out_pair, gains, up_pair, down_pair, slope_pair, tile=256, chunk=768):
    rows, width = x.shape
    local_ff = up_pair[0].shape[1]
    steps = local_ff // chunk
    shape = jax.ShapeDtypeStruct
    cols = lambda height: [first_cols(height, chunk, steps), second_cols(height, chunk, steps)]
    return pl.pallas_call(
        functools.partial(late_kernel, tile=tile, steps=steps),
        grid=(2 * steps,),
        in_specs=[once(x), once(mixed), once(cot), once(spread), once(out_pair[0]), once(out_pair[1]), once(gains)]
        + cols(width) * 2
        + cols(rows),
        out_specs=[once(x), once(x), whole_shape((8, width))] + cols(width),
        out_shape=[shape((rows, width), BF16)] * 2 + [shape((8, width), F32)] + [shape((width, local_ff), BF16)] * 2,
        scratch_shapes=[
            pltpu.VMEM((width, rows), BF16),
            pltpu.VMEM((rows, width), BF16),
            pltpu.VMEM((rows, width), F32),
            pltpu.VMEM((rows, width), F32),
            pltpu.VMEM((rows, chunk), BF16),
        ],
        compiler_params=params(48),
        cost_estimate=cost(4 * rows * width * (width + 3 * local_ff), rows * (width * 10 + local_ff * 4) + width * (width + local_ff * 6) * 2),
        name="late_part",
    )(x, mixed, cot, spread, *out_pair, gains, *up_pair, *down_pair, *slope_pair)


def blank(*likes):
    return pl.pallas_call(
        lambda *refs: None,
        out_specs=[pl.BlockSpec(memory_space=pl.ANY)] * len(likes),
        out_shape=[jax.ShapeDtypeStruct(shape, dtype) for shape, dtype in likes],
        compiler_params=params(4),
        name="blank",
    )()


def input_kernel(
    x_ref, normed_ref, attn_ref, mixed_ref, d_own, d_oth, w_own, w_oth, gain_ref,
    out_ref, gain_grad_ref, g_own, g_oth, total_ref, normed_t, attn_t, *, tile, steps
):
    index = pl.program_id(0)
    width = x_ref.shape[1]
    half = width // 2
    tiles = row_tiles(x_ref.shape[0], tile)

    @pl.when(index == 0)
    def _():
        total_ref[...] = jnp.zeros_like(total_ref)
        for at in tiles:
            normed_t[:, at] = normed_ref[at].T
            attn_t[:, at] = attn_ref[at].T

    def run(d_ref, w_ref, g_ref):
        for at in tiles:
            total_ref[at] += dot(d_ref[at], w_ref[...], 1, 1)
        for at in row_tiles(width, tile):
            g_ref[at] = dot(normed_t[at], d_ref[...], 1, 0).astype(BF16)

    def run_out(cols, g_ref):
        for at in row_tiles(width, tile):
            g_ref[at] = dot(attn_t[at], mixed_ref[:, cols], 1, 0).astype(BF16)

    pl.when(index < steps)(lambda: run(d_own, w_own, g_own))
    pl.when(index == steps)(lambda: run_out(slice(0, half), g_own))
    pl.when((index > steps) & (index <= 2 * steps))(lambda: run(d_oth, w_oth, g_oth))

    @pl.when(index == 2 * steps + 1)
    def _():
        run_out(slice(half, width), g_oth)
        gain_total = jnp.zeros((1, width), F32)
        for at in tiles:
            part, gain_part = norm_back(x_ref[at].astype(F32), total_ref[at], gain_ref[0:1])
            gain_total = gain_total + gain_part
            out_ref[at] = (attn_ref[at].astype(F32) + part).astype(BF16)
        gain_grad_ref[...] = jnp.broadcast_to(gain_total, gain_grad_ref.shape)


def input_back(x, normed, attn_low, mixed, d_pair, w_pair, gains, tile=256):
    rows, width = x.shape
    wide = d_pair[0].shape[1]
    chunk = width // 2
    steps = wide // chunk
    shape = jax.ShapeDtypeStruct
    at_own = lambda height: pl.BlockSpec((height, chunk), lambda i: (0, jnp.minimum(i, steps - 1)))
    at_oth = lambda height: pl.BlockSpec((height, chunk), lambda i: (0, jnp.clip(i - steps - 1, 0, steps - 1)))
    return pl.pallas_call(
        functools.partial(input_kernel, tile=tile, steps=steps),
        grid=(2 * steps + 2,),
        in_specs=[once(x), once(x), once(x), once(x), at_own(rows), at_oth(rows), at_own(width), at_oth(width), once(gains)],
        out_specs=[once(x), whole_shape((8, width)), first_cols(width, chunk, steps + 1), second_cols(width, chunk, steps + 1)],
        out_shape=[shape((rows, width), BF16), shape((8, width), F32)] + [shape((width, wide + chunk), BF16)] * 2,
        scratch_shapes=[
            pltpu.VMEM((rows, width), F32),
            pltpu.VMEM((width, rows), BF16),
            pltpu.VMEM((width, rows), BF16),
        ],
        compiler_params=params(32),
        cost_estimate=cost(8 * rows * width * wide + 2 * rows * width * width, rows * (width * 10 + wide * 4) + width * wide * 8),
        name="qkv_back",
    )(x, normed, attn_low, mixed, *d_pair, *w_pair, gains)


def crossed():
    return lax.axis_index("half") != lax.axis_index("mp")


def swap_in(value):
    return lax.ppermute(value, ("half", "mp"), [(1, 2), (2, 1)])


def swapped(value):
    return jnp.where(crossed(), swap_in(value), value)


def from_mate(value):
    return lax.ppermute(value, "half", [(0, 1), (1, 0)])


def along_dp(value, bit):
    return lax.ppermute(value, "dp", [(i, i ^ bit) for i in range(8)])


def pick(value, index, axis=0):
    return lax.dynamic_index_in_dim(value, index, axis, keepdims=False)


def neighbours_swap(value):
    shards, split = lax.axis_size("dp"), lax.axis_size("mp")
    pairs = [
        ((h * shards + d) * split + m, (h * shards + (d ^ 1)) * split + m)
        for h in range(2)
        for d in range(shards)
        for m in range(split)
        if h != m
    ]
    return lax.ppermute(value, ("half", "dp", "mp"), pairs)


def after(value, *others):
    return lax.optimization_barrier((value, *others))[0]


def fetch(weight, gate=None, mate_gate=None):
    received = swap_in(weight if gate is None else after(weight, gate))
    own = jnp.where(crossed(), received if mate_gate is None else after(received, mate_gate), weight)
    return own, from_mate(own), received


def fetch_shared(weight, gate, pass_gate):
    rows, cols = weight.shape
    parts = weight.reshape(2, rows // 2, cols)
    odd = lax.axis_index("dp") % 2
    mine = swap_in(after(pick(parts, odd), gate))
    other = neighbours_swap(after(mine, pass_gate))
    got = jnp.where(odd == 0, jnp.stack([mine, other]), jnp.stack([other, mine]))
    own = jnp.where(crossed(), got, parts).reshape(rows, cols)
    return own, from_mate(own), mine


def low_sum(one, two):
    return (one.astype(F32) + two.astype(F32)).astype(BF16)


def x_summed(grad, *gate):
    if lax.axis_size("dp") != 8:
        return grad
    rows, cols = grad.shape
    odd = lax.axis_index("dp") % 2
    view = grad.reshape(4, 2, rows // 8, cols)
    got = along_dp(after(pick(view, 1 - odd, 1), *gate), 1)
    return low_sum(pick(view, odd, 1), got)


def z_summed(part, *gate):
    if lax.axis_size("dp") != 8:
        return lax.psum_scatter(part.astype(F32), "dp", scatter_dimension=0, tiled=True)
    at = lax.axis_index("dp") // 2
    view = part.reshape(2, 2, *part.shape[1:])
    got = along_dp(after(pick(view, 1 - at % 2, 1), *gate), 2)
    view = low_sum(pick(view, at % 2, 1), got)
    got = along_dp(pick(view, 1 - at // 2), 4)
    return pick(view, at // 2).astype(F32) + got.astype(F32)


def all_sum(value):
    shards = lax.axis_size("dp")
    if shards != 8:
        return lax.psum(value, ("half", "dp"))
    value = value + from_mate(value)
    for bit in (1, 2, 4):
        value = value + along_dp(value, bit)
    return value


def body(tokens, norm_gains, qkv_w, out_w, up_w, down_w, memory, memory_ids, counts, prefix_mask, cotangent):
    core = lax.axis_index("half")
    layer = lax.axis_index("mp")
    shard_count = lax.axis_size("dp")
    shard_index = lax.axis_index("dp")
    rows, width = tokens.shape[1:]
    questions, k_most = memory_ids.shape
    mem_dev = memory.shape[1]
    score_scale = (4 * width) ** (-0.5)
    local_hd = qkv_w.shape[3]
    padded = 16

    gains = swapped(norm_gains[0])
    x_in = swap_in(tokens[0])
    x = jnp.where(crossed(), x_in, tokens[0])
    *qkv_pair, qkv_in = fetch(qkv_w[0].reshape(width, 3 * local_hd))
    normed, *proj = project(x, gains, qkv_pair)
    *out_pair, _ = fetch(out_w[0], x_in, proj[0])
    *up_pair, up_in = fetch_shared(up_w[0], x_in, proj[0])
    self_mixed = attention(*proj)
    *down_pair, down_in = fetch(down_w[0], qkv_in, self_mixed)
    cot = swapped(after(cotangent[0], down_in))

    slot_total = questions * k_most
    capacity = (slot_total + shard_count - 1) // shard_count
    table = memory[0].reshape(mem_dev, 4 * width)
    local_rows = jnp.concatenate(
        [memory_ids.reshape(-1) % mem_dev, jnp.zeros((capacity * shard_count - slot_total,), jnp.int32)]
    )
    requests = jnp.roll(local_rows.reshape(capacity, shard_count), shard_index, axis=1).T
    asked = lax.all_to_all(requests, "dp", split_axis=0, concat_axis=0, tiled=True).reshape(-1)
    answer = dot((asked[:, None] == jnp.arange(mem_dev)[None, :]).astype(BF16), table, 1, 0).astype(BF16)
    answers = lax.all_to_all(answer, "dp", split_axis=0, concat_axis=0, tiled=True)
    answers = swapped(after(answers, up_in))
    at = jnp.arange(questions * padded)
    slot = at % padded
    flat = at // padded * k_most + slot
    source = (shard_index + flat % shard_count) % shard_count * capacity + flat // shard_count
    source = jnp.where(slot < k_most, source, -1)
    chosen = (source[:, None] == jnp.arange(capacity * shard_count)[None, :]).astype(BF16)
    found = dot(chosen, answers, 1, 0).astype(BF16)
    half = width // 2
    other_way = jnp.concatenate(
        [found[:, c * width + h * half : c * width + (h + 1) * half] for c in range(4) for h in (1, 0)], axis=1
    )
    found_heads = jnp.where(core == 0, found, other_way).reshape(questions, padded, 4 * width)
    found = found.reshape(questions, padded, 4 * width)

    valid = (jnp.arange(k_most)[None, :] < counts[:, None])[:, None, :] & (
        jnp.swapaxes(prefix_mask.reshape(questions, k_most, 2), 1, 2) == 1
    )
    valid = jnp.pad(valid.astype(F32), ((0, 0), (0, 0), (0, padded - k_most))).reshape(questions, 2 * padded)
    valid = (swapped(valid) > 0.5) & (layer == 1)

    def biases(scores):
        wide = jnp.tile(jnp.pad(scores.astype(F32), ((0, 0), (0, padded - k_most))), (1, 2))
        bias = jnp.where(valid, wide, MASKED)
        return jnp.broadcast_to(bias[:, :, None], (questions, 2 * padded, LANES))

    joining = layer == 1
    pooled = pooled_result(x, self_mixed, out_pair, gains, up_pair, down_pair)
    pooled = (pooled * (1.0 / RUN)).reshape(questions, 4 * width)
    scores = jnp.sum(pooled[:, None, :] * found[:, :k_most].astype(F32), axis=-1) * score_scale
    sent = lax.ppermute(scores.astype(BF16), "mp", [(0, 1)])

    bias = biases(sent)
    local_ff = up_w.shape[2]
    tall = ((rows, local_ff), BF16)
    flat = ((rows, width), BF16)
    grad_like = ((width, local_ff), BF16)
    run_like = ((rows // RUN, local_ff), BF16)
    slot_like = ((questions, 2 * padded, LANES), F32)
    gain_like = ((8, width), F32)

    def join_first():
        mixed = attention(*proj, (found_heads, bias))
        attn_low, mgrad, gain_two, hid_own, hid_oth, pre_own, pre_oth = join_part(
            x, mixed, cot, out_pair, gains, up_pair, down_pair
        )
        slots = slot_sums(*proj, found_heads, bias, mgrad)
        unused = blank(grad_like, grad_like, run_like, run_like)
        return mixed, attn_low, mgrad, gain_two, hid_own, hid_oth, pre_own, pre_oth, slots, *unused

    def key_first():
        result, slope_own, slope_oth, *rest = early_part(x, self_mixed, cot, out_pair, gains, up_pair, down_pair)
        mgrad, gain_two, pre_own, pre_oth, slots = blank(flat, gain_like, tall, tall, slot_like)
        return self_mixed, result, mgrad, gain_two, slope_own, slope_oth, pre_own, pre_oth, slots, *rest

    (mixed, flat_one, mgrad, gain_two, tall_own, tall_oth, pre_own, pre_oth, slots, *key_down, run_own, run_oth) = lax.cond(
        joining, join_first, key_first
    )
    slot_grad = slots[:, :, 0]
    score_low = (slot_grad[:, :k_most] + slot_grad[:, padded : padded + k_most]).astype(BF16)
    score_in = lax.ppermute(score_low, "mp", [(1, 0)])

    scale = score_scale / RUN
    spread = jnp.sum(
        (score_in.astype(F32) * scale)[:, :, None] * found[:, :k_most].astype(F32), axis=1
    ).reshape(rows // RUN, width)

    def weight_grad(rows_of, cols_of, base=0.0):
        return (dot(rows_of, cols_of, 0, 0) + base).astype(BF16)

    def join_down():
        return weight_grad(cot, tall_own), weight_grad(cot, tall_oth)

    def key_down_all():
        spread_low = spread.astype(BF16)
        return tuple(
            weight_grad(spread_low, r, g.astype(F32)) for g, r in zip(key_down, (run_own, run_oth))
        )

    down_own, down_oth = lax.cond(joining, join_down, key_down_all)
    down_grad = low_sum(down_own, from_mate(down_oth))

    def join_second():
        result, up_own, up_oth = join_grads(
            x, mixed, out_pair, gains, down_pair, (tall_own, tall_oth), (pre_own, pre_oth)
        )
        return result, flat_one, mgrad, gain_two, up_own, up_oth

    def key_second():
        return flat_one, *late_part(
            x, mixed, cot, spread, out_pair, gains, up_pair, down_pair, (tall_own, tall_oth)
        )

    result, attn_low, mgrad, gain_two, up_own, up_oth = lax.cond(joining, join_second, key_second)
    up_grad = low_sum(up_own, from_mate(up_oth))
    down_part = x_summed(down_grad)
    d_own, d_oth, _ = attention_back(*proj, found_heads, bias, after(mgrad, down_grad))
    up_part = x_summed(up_grad, down_part)
    grad_in, gain_one, head_own, head_oth = input_back(
        x, normed, attn_low, mixed, (after(d_own, up_grad), d_oth), qkv_pair, gains
    )
    head_part = x_summed(low_sum(head_own, from_mate(head_oth)), up_part)

    def placed(sum_rows):
        return swapped(sum_rows.astype(BF16)).astype(F32)

    down_g, up_g, head_g = (placed(z_summed(part)) for part in (down_part, up_part, head_part))
    gain_grads = swapped(all_sum(jnp.concatenate([gain_one[:1], gain_two[:1]], axis=0)))
    activations = swapped(result)
    input_grad = swapped(grad_in).astype(F32)
    score_out = swapped(jnp.where(joining, score_low, score_in)).astype(F32)
    return (
        activations[None],
        input_grad[None],
        score_out,
        gain_grads[None],
        head_g[:, : 3 * local_hd].reshape(1, -1, 3, local_hd),
        head_g[None, :, 3 * local_hd :],
        up_g[None],
        down_g[None],
    )


def solution(mesh):
    placed = (
        P("half", ("dp", "mp"), None),
        P("half", None, None),
        P("half", None, None, "mp"),
        P("half", None, "mp"),
        P("half", None, "mp"),
        P("half", None, "mp"),
        P("half", "dp", None, None),
        P(("dp", "mp"), None),
        P(("dp", "mp")),
        P(("dp", "mp"), None),
        P("half", ("dp", "mp"), None),
    )
    return jax.shard_map(
        body,
        mesh=mesh,
        in_specs=placed,
        out_specs=(
            P("half", ("dp", "mp"), None),
            P("half", ("dp", "mp"), None),
            P(("dp", "mp"), None),
            P("half", None, None),
            P("half", "dp", None, "mp"),
            P("half", "dp", "mp"),
            P("half", "dp", "mp"),
            P("half", "dp", "mp"),
        ),
        check_vma=False,
    )
```

```python
import functools

import jax
import jax.numpy as jnp
from jax import lax
from jax.experimental import pallas as pl
from jax.experimental.pallas import tpu as pltpu
from jax.sharding import PartitionSpec as P

HDIM = 64
QLEN = 64
RUN = 16
LANES = 128
NORM_EPS = 1e-06
MASKED = -1e30
F32 = jnp.float32
BF16 = jnp.bfloat16
GELU_A = 0.7978845608028654
GELU_B = 0.044715 * GELU_A


def dot(a, b, ca, cb):
    return lax.dot_general(a, b, (((ca,), (cb,)), ((), ())), preferred_element_type=F32)


def params(mebibytes):
    return pltpu.CompilerParams(vmem_limit_bytes=mebibytes << 20)


def cost(flops, nbytes, trans=0):
    return pl.CostEstimate(flops=int(flops), bytes_accessed=int(nbytes), transcendentals=int(trans))


def head_stack(block):
    lane = lax.broadcasted_iota(jnp.int32, block.shape, 1)
    zero = jnp.zeros_like(block)
    return jnp.concatenate(
        [jnp.where(lane < HDIM, block, zero), jnp.where(lane < HDIM, zero, block)], axis=0
    )


def head_merge(stacked):
    lane = lax.broadcasted_iota(jnp.int32, (QLEN, LANES), 1)
    return jnp.where(lane < HDIM, stacked[:QLEN], stacked[QLEN:])


def pair_views(own_ref, oth_ref, found_ref, question, pair, local_hd, width):
    ref = own_ref if pair * LANES < local_hd else oth_ref
    base = pair * LANES % local_hd
    rows = slice(question * QLEN, (question + 1) * QLEN)
    query = ref[rows, base : base + LANES]
    key = ref[rows, local_hd + base : local_hd + base + LANES]
    value = ref[rows, 2 * local_hd + base : 2 * local_hd + base + LANES]
    stack = head_stack(query * jnp.asarray(HDIM**-0.5, BF16))
    if found_ref is None:
        return stack, key, value
    col = pair * LANES
    pref = [found_ref[question, :, c * width + col : c * width + col + LANES] for c in range(4)]
    keys = jnp.concatenate([key, pref[0], pref[1]], axis=0)
    values = jnp.concatenate([value, pref[2], pref[3]], axis=0)
    return stack, keys, values


def pair_logits(stack, keys, bias):
    logits = dot(keys, stack, 1, 1)
    if bias is None:
        return logits
    return jnp.concatenate([logits[:QLEN], logits[QLEN:] + bias], axis=0)


def softmax_down(logits):
    weights = jnp.exp(logits - jnp.max(logits, axis=0, keepdims=True))
    return weights * (1.0 / jnp.sum(weights, axis=0, keepdims=True))


def grouped(questions, pairs, group):
    items = [(question, pair) for question in range(questions) for pair in range(pairs)]
    return [items[at : at + group] for at in range(0, len(items), group)]


def attention_kernel(own_ref, oth_ref, *refs, questions, local_hd, width, group):
    found_ref, bias_ref, mixed_ref = refs if len(refs) == 3 else (None, None, *refs)
    for items in grouped(questions, width // LANES, group):
        views = [pair_views(own_ref, oth_ref, found_ref, q, p, local_hd, width) for q, p in items]
        logits = [pair_logits(v[0], v[1], None if bias_ref is None else bias_ref[q]) for v, (q, p) in zip(views, items)]
        probs = [softmax_down(l).astype(BF16) for l in logits]
        mixed = [dot(p, v[2], 0, 0) for p, v in zip(probs, views)]
        for m, (q, p) in zip(mixed, items):
            mixed_ref[q * QLEN : (q + 1) * QLEN, p * LANES : (p + 1) * LANES] = head_merge(m).astype(BF16)


def attention(own, oth, prefix=(), questions=4, group=12):
    rows, local_hd = own.shape[0], own.shape[1] // 3
    width = 2 * local_hd
    count = rows // QLEN
    block = questions * QLEN
    return pl.pallas_call(
        functools.partial(attention_kernel, questions=questions, local_hd=local_hd, width=width, group=group),
        grid=(count // questions,),
        in_specs=[pl.BlockSpec((block, 3 * local_hd), lambda i: (i, 0))] * 2
        + [pl.BlockSpec((questions, *a.shape[1:]), lambda i: (i, 0, 0)) for a in prefix],
        out_specs=pl.BlockSpec((block, width), lambda i: (i, 0)),
        out_shape=jax.ShapeDtypeStruct((rows, width), BF16),
        compiler_params=params(20),
        cost_estimate=cost(rows * width * 96 * 8, rows * width * 8, rows * 12 * 96),
        name="attend",
    )(own, oth, *prefix)


def attention_back_kernel(
    own_ref, oth_ref, found_ref, bias_ref, mixed_ref, down_ref, doth_ref, slot_ref, *, questions, local_hd, width, group
):
    totals = [None] * questions
    for items in grouped(questions, width // LANES, group):
        views = [pair_views(own_ref, oth_ref, found_ref, q, p, local_hd, width) for q, p in items]
        logits = [pair_logits(v[0], v[1], bias_ref[q]) for v, (q, p) in zip(views, items)]
        grads = [
            head_stack(mixed_ref[q * QLEN : (q + 1) * QLEN, p * LANES : (p + 1) * LANES]) for q, p in items
        ]
        prob_grads = [dot(v[2], g, 1, 1) for v, g in zip(views, grads)]
        probs = [softmax_down(l) for l in logits]
        deltas = [jnp.sum(p * g, axis=0, keepdims=True) for p, g in zip(probs, prob_grads)]
        logit_grads = [p * (g - d) for p, g, d in zip(probs, prob_grads, deltas)]
        lows = [l.astype(BF16) for l in logit_grads]
        value_grads = [dot(p[:QLEN].astype(BF16), g, 1, 0) for p, g in zip(probs, grads)]
        key_grads = [dot(l[:QLEN], v[0], 1, 0) for l, v in zip(lows, views)]
        query_grads = [dot(l, v[1], 0, 0) for l, v in zip(lows, views)]
        for at, (q, p) in enumerate(items):
            part = logit_grads[at][QLEN:]
            totals[q] = part if totals[q] is None else totals[q] + part
            out = down_ref if p * LANES < local_hd else doth_ref
            base = p * LANES % local_hd
            rows = slice(q * QLEN, (q + 1) * QLEN)
            out[rows, base : base + LANES] = (head_merge(query_grads[at]) * HDIM**-0.5).astype(BF16)
            out[rows, local_hd + base : local_hd + base + LANES] = key_grads[at].astype(BF16)
            out[rows, 2 * local_hd + base : 2 * local_hd + base + LANES] = value_grads[at].astype(BF16)
    for q in range(questions):
        slot_ref[q] = jnp.broadcast_to(jnp.sum(totals[q], axis=1, keepdims=True), totals[q].shape)


def attention_back(own, oth, found, bias, mixed_low, questions=2, group=12):
    rows, local_hd = own.shape[0], own.shape[1] // 3
    width = 2 * local_hd
    count = rows // QLEN
    slots = found.shape[1]
    block = questions * QLEN
    wide = pl.BlockSpec((block, 3 * local_hd), lambda i: (i, 0))
    bias_spec = pl.BlockSpec((questions, 2 * slots, LANES), lambda i: (i, 0, 0))
    return pl.pallas_call(
        functools.partial(
            attention_back_kernel, questions=questions, local_hd=local_hd, width=width, group=group
        ),
        grid=(count // questions,),
        in_specs=[
            wide,
            wide,
            pl.BlockSpec((questions, slots, 4 * width), lambda i: (i, 0, 0)),
            bias_spec,
            pl.BlockSpec((block, width), lambda i: (i, 0)),
        ],
        out_specs=[wide, wide, bias_spec],
        out_shape=[
            jax.ShapeDtypeStruct((rows, 3 * local_hd), BF16),
            jax.ShapeDtypeStruct((rows, 3 * local_hd), BF16),
            jax.ShapeDtypeStruct((count, 2 * slots, LANES), F32),
        ],
        compiler_params=params(24),
        cost_estimate=cost(rows * width * 96 * 20, rows * width * 16, rows * 12 * 96),
        name="attend_back",
    )(own, oth, found, bias, mixed_low)


def slot_kernel(own_ref, oth_ref, found_ref, bias_ref, mixed_ref, slot_ref, *, questions, local_hd, width, group):
    totals = [None] * questions
    for items in grouped(questions, width // LANES, group):
        views = [pair_views(own_ref, oth_ref, found_ref, q, p, local_hd, width) for q, p in items]
        logits = [pair_logits(v[0], v[1], bias_ref[q]) for v, (q, p) in zip(views, items)]
        grads = [
            head_stack(mixed_ref[q * QLEN : (q + 1) * QLEN, p * LANES : (p + 1) * LANES]) for q, p in items
        ]
        prob_grads = [dot(v[2], g, 1, 1) for v, g in zip(views, grads)]
        probs = [softmax_down(l) for l in logits]
        deltas = [jnp.sum(p * g, axis=0, keepdims=True) for p, g in zip(probs, prob_grads)]
        parts = [p[QLEN:] * (g[QLEN:] - d) for p, g, d in zip(probs, prob_grads, deltas)]
        for part, (q, p) in zip(parts, items):
            totals[q] = part if totals[q] is None else totals[q] + part
    for q in range(questions):
        slot_ref[q] = jnp.broadcast_to(jnp.sum(totals[q], axis=1, keepdims=True), totals[q].shape)


def slot_sums(own, oth, found, bias, mixed_low, questions=4, group=12):
    rows, local_hd = own.shape[0], own.shape[1] // 3
    width = 2 * local_hd
    count = rows // QLEN
    slots = found.shape[1]
    block = questions * QLEN
    wide = pl.BlockSpec((block, 3 * local_hd), lambda i: (i, 0))
    bias_spec = pl.BlockSpec((questions, 2 * slots, LANES), lambda i: (i, 0, 0))
    return pl.pallas_call(
        functools.partial(slot_kernel, questions=questions, local_hd=local_hd, width=width, group=group),
        grid=(count // questions,),
        in_specs=[
            wide,
            wide,
            pl.BlockSpec((questions, slots, 4 * width), lambda i: (i, 0, 0)),
            bias_spec,
            pl.BlockSpec((block, width), lambda i: (i, 0)),
        ],
        out_specs=bias_spec,
        out_shape=jax.ShapeDtypeStruct((count, 2 * slots, LANES), F32),
        compiler_params=params(20),
        cost_estimate=cost(rows * width * 96 * 8, rows * width * 12, rows * 12 * 96),
        name="slot_sums",
    )(own, oth, found, bias, mixed_low)


def rms_scale(block):
    return lax.rsqrt(jnp.mean(block * block, axis=-1, keepdims=True) + NORM_EPS)


def row_tiles(rows, tile):
    return rows, tile


def each(tiles, unrolled=False):
    rows, tile = tiles

    def loop(body):
        if unrolled:
            for at in range(0, rows, tile):
                body(slice(at, at + tile))
            return

        @pl.loop(0, rows // tile)
        def _(step):
            body(pl.ds(pl.multiple_of(step * tile, tile), tile))

    return loop


def whole(array):
    return pl.BlockSpec(array.shape, lambda i: (0,) * array.ndim)


def whole_shape(shape):
    return pl.BlockSpec(shape, lambda i: (0, 0))


def first_cols(rows, chunk, steps):
    return pl.BlockSpec((rows, chunk), lambda i: (0, jnp.minimum(i, steps - 1)))


def second_cols(rows, chunk, steps):
    return pl.BlockSpec((rows, chunk), lambda i: (0, jnp.maximum(i - steps, 0)))


def by_half(steps, first, second):
    index = pl.program_id(0)
    pl.when(index < steps)(first)
    pl.when(index >= steps)(second)


def project_kernel(x_ref, gain_ref, w_own, w_oth, normed_ref, own_ref, oth_ref, *, tile, steps):
    tiles = row_tiles(x_ref.shape[0], tile)

    @pl.when(pl.program_id(0) == 0)
    def _():
        @each(tiles, True)
        def _(at):
            block = x_ref[at].astype(F32)
            normed_ref[at] = (block * rms_scale(block) * gain_ref[0:1]).astype(BF16)

    def run(w_ref, out_ref):
        @each(tiles, True)
        def _(at):
            out_ref[at] = dot(normed_ref[at], w_ref[...], 1, 0).astype(BF16)

    by_half(steps, lambda: run(w_own, own_ref), lambda: run(w_oth, oth_ref))


def project(x, gains, w_pair, tile=256, chunk=384):
    rows, width = x.shape
    cols = w_pair[0].shape[1]
    steps = cols // chunk
    shape = jax.ShapeDtypeStruct
    return pl.pallas_call(
        functools.partial(project_kernel, tile=tile, steps=steps),
        grid=(2 * steps,),
        in_specs=[whole(x), whole(gains), first_cols(width, chunk, steps), second_cols(width, chunk, steps)],
        out_specs=[whole(x), first_cols(rows, chunk, steps), second_cols(rows, chunk, steps)],
        out_shape=[shape((rows, width), BF16), shape((rows, cols), BF16), shape((rows, cols), BF16)],
        compiler_params=params(24),
        cost_estimate=cost(4 * rows * width * cols, rows * (width + cols) * 4 + width * cols * 4),
        name="project",
    )(x, gains, *w_pair)


def norm_back(block, grad, gain):
    scale = rms_scale(block)
    weighted = grad * gain
    inner = jnp.mean(block * weighted, axis=-1, keepdims=True)
    return (
        scale * weighted - block * (scale * scale * scale * inner),
        jnp.sum(grad * block * scale, axis=0, keepdims=True),
    )


def gelu_terms(pre):
    cube = GELU_B * (pre * pre)
    return cube, jnp.tanh(pre * (GELU_A + cube)), 0.5 * pre


def gelu_value(terms):
    _, bend, half_pre = terms
    return half_pre * bend + half_pre


def gelu_slope(terms):
    cube, bend, half_pre = terms
    return (0.5 + 0.5 * bend) + half_pre * (1.0 - bend * bend) * (GELU_A + 3.0 * cube)


def residual_rows(at, x_ref, mixed_ref, out_own, out_oth):
    half = mixed_ref.shape[1] // 2
    return (
        x_ref[at].astype(F32)
        + dot(mixed_ref[at, :half], out_own[...], 1, 1)
        + dot(mixed_ref[at, half:], out_oth[...], 1, 1)
    )


def normed_rows(residual, gain):
    return (residual * rms_scale(residual) * gain).astype(BF16)


def score_kernel(
    x_ref, mixed_ref, out_own, out_oth, gain_ref, up_own, up_oth, down_own, down_oth,
    pooled_ref, normed_ref, total_ref, *, tile, steps
):
    index = pl.program_id(0)
    tiles = row_tiles(x_ref.shape[0], tile)

    @pl.when(index == 0)
    def _():
        @each(tiles, True)
        def _(at):
            residual = residual_rows(at, x_ref, mixed_ref, out_own, out_oth)
            total_ref[at] = residual
            normed_ref[at] = normed_rows(residual, gain_ref[1:2])

    def run(up_ref, down_ref):
        @each(tiles, True)
        def _(at):
            hidden = gelu_value(gelu_terms(dot(normed_ref[at], up_ref[...], 1, 0))).astype(BF16)
            total_ref[at] += dot(hidden, down_ref[...], 1, 1)

    by_half(steps, lambda: run(up_own, down_own), lambda: run(up_oth, down_oth))

    @pl.when(index == 2 * steps - 1)
    def _():
        @each(tiles, True)
        def _(at):
            result = total_ref[at]
            runs = slice(at.start // RUN, at.stop // RUN)
            pooled_ref[runs] = jnp.sum(result.reshape(tile // RUN, RUN, result.shape[1]), axis=1)


def once(array):
    return pl.BlockSpec(array.shape, lambda i: (0,) * array.ndim, pipeline_mode=pl.Buffered(1))


def pooled_result(x, mixed, out_pair, gains, up_pair, down_pair, tile=256, chunk=768):
    rows, width = x.shape
    local_ff = up_pair[0].shape[1]
    steps = local_ff // chunk
    cols = [first_cols(width, chunk, steps), second_cols(width, chunk, steps)]
    return pl.pallas_call(
        functools.partial(score_kernel, tile=tile, steps=steps),
        grid=(2 * steps,),
        in_specs=[once(x), once(mixed), once(out_pair[0]), once(out_pair[1]), once(gains)] + cols * 2,
        out_specs=whole_shape((rows // RUN, width)),
        out_shape=jax.ShapeDtypeStruct((rows // RUN, width), F32),
        scratch_shapes=[pltpu.VMEM((rows, width), BF16), pltpu.VMEM((rows, width), F32)],
        compiler_params=params(30),
        cost_estimate=cost(2 * rows * width * (width + 4 * local_ff), rows * width * 4 + width * (width + local_ff * 4) * 2, rows * local_ff * 2),
        name="pooled_result",
    )(x, mixed, *out_pair, gains, *up_pair, *down_pair)


def early_kernel(
    x_ref, mixed_ref, cot_ref, out_own, out_oth, gain_ref, up_own, up_oth, down_own, down_oth,
    result_ref, slope_own, slope_oth, grad_own, grad_oth, run_own, run_oth,
    normed_ref, sum_ref, left_ref, hid_ref, *, tile, steps
):
    index = pl.program_id(0)
    rows, width = x_ref.shape
    runs = rows // RUN
    tiles = row_tiles(rows, tile)

    @pl.when(index == 0)
    def _():
        @each(tiles)
        def _(at):
            residual = residual_rows(at, x_ref, mixed_ref, out_own, out_oth)
            sum_ref[at] = residual
            normed_ref[at] = normed_rows(residual, gain_ref[1:2])
            left_ref[:width, at] = cot_ref[at].T
        run_of = lax.broadcasted_iota(jnp.int32, (runs, rows), 0) * RUN
        row_at = lax.broadcasted_iota(jnp.int32, (runs, rows), 1)
        left_ref[width:] = jnp.where((row_at >= run_of) & (row_at < run_of + RUN), 1.0, 0.0).astype(BF16)

    def run(up_ref, down_ref, slope_ref, grad_ref, run_ref):
        @each(tiles)
        def _(at):
            terms = gelu_terms(dot(normed_ref[at], up_ref[...], 1, 0))
            hidden = gelu_value(terms).astype(BF16)
            hid_ref[at] = hidden
            slope_ref[at] = gelu_slope(terms).astype(BF16)
            sum_ref[at] += dot(hidden, down_ref[...], 1, 1)
        @each(row_tiles(width, width // 2))
        def _(at):
            grad_ref[at] = dot(left_ref[at], hid_ref[...], 1, 0).astype(BF16)
        run_ref[...] = dot(left_ref[width:], hid_ref[...], 1, 0).astype(BF16)

    by_half(
        steps,
        lambda: run(up_own, down_own, slope_own, grad_own, run_own),
        lambda: run(up_oth, down_oth, slope_oth, grad_oth, run_oth),
    )

    @pl.when(index == 2 * steps - 1)
    def _():
        @each(tiles)
        def _(at):
            result_ref[at] = sum_ref[at].astype(BF16)


def early_part(x, mixed, cot, out_pair, gains, up_pair, down_pair, tile=512, chunk=512):
    rows, width = x.shape
    local_ff = up_pair[0].shape[1]
    runs = rows // RUN
    steps = local_ff // chunk
    shape = jax.ShapeDtypeStruct
    cols = lambda height: [first_cols(height, chunk, steps), second_cols(height, chunk, steps)]
    return pl.pallas_call(
        functools.partial(early_kernel, tile=tile, steps=steps),
        grid=(2 * steps,),
        in_specs=[once(x), once(mixed), once(cot), once(out_pair[0]), once(out_pair[1]), once(gains)] + cols(width) * 2,
        out_specs=[once(x)] + cols(rows) + cols(width) + cols(runs),
        out_shape=[shape((rows, width), BF16)]
        + [shape((rows, local_ff), BF16)] * 2
        + [shape((width, local_ff), BF16)] * 2
        + [shape((runs, local_ff), BF16)] * 2,
        scratch_shapes=[
            pltpu.VMEM((rows, width), BF16),
            pltpu.VMEM((rows, width), F32),
            pltpu.VMEM((width + runs, rows), BF16),
            pltpu.VMEM((rows, chunk), BF16),
        ],
        compiler_params=params(40),
        cost_estimate=cost(2 * rows * width * (width + 6 * local_ff), rows * (width * 8 + local_ff * 4) + width * (width + local_ff * 6) * 2, rows * local_ff * 2),
        name="early_part",
    )(x, mixed, cot, *out_pair, gains, *up_pair, *down_pair)


def finish_rows(tiles, grad_of, resid_ref, total_ref, gain_ref, out_own, out_oth, attn_ref, mgrad_ref, gain_grad_ref):
    half = out_own.shape[1]
    gain_grad_ref[...] = jnp.zeros_like(gain_grad_ref)

    @each(tiles)
    def _(at):
        part, gain_part = norm_back(resid_ref[at], total_ref[at], gain_ref[1:2])
        gain_grad_ref[0:1] += gain_part
        attn_low = (grad_of(at) + part).astype(BF16)
        attn_ref[at] = attn_low
        mgrad_ref[at, :half] = dot(attn_low, out_own[...], 1, 0).astype(BF16)
        mgrad_ref[at, half:] = dot(attn_low, out_oth[...], 1, 0).astype(BF16)


def join_kernel(
    x_ref, mixed_ref, cot_ref, out_own, out_oth, gain_ref, up_own, up_oth, down_own, down_oth,
    attn_ref, mgrad_ref, gain_grad_ref, hid_own, hid_oth, pre_own, pre_oth,
    normed_ref, resid_ref, total_ref, *, tile, steps
):
    index = pl.program_id(0)
    tiles = row_tiles(x_ref.shape[0], tile)

    @pl.when(index == 0)
    def _():
        total_ref[...] = jnp.zeros_like(total_ref)
        @each(tiles)
        def _(at):
            residual = residual_rows(at, x_ref, mixed_ref, out_own, out_oth)
            resid_ref[at] = residual
            normed_ref[at] = normed_rows(residual, gain_ref[1:2])

    def run(up_ref, down_ref, hid_ref, pre_ref):
        @each(tiles)
        def _(at):
            terms = gelu_terms(dot(normed_ref[at], up_ref[...], 1, 0))
            hid_ref[at] = gelu_value(terms).astype(BF16)
            pre_low = (dot(cot_ref[at], down_ref[...], 1, 0) * gelu_slope(terms)).astype(BF16)
            pre_ref[at] = pre_low
            total_ref[at] += dot(pre_low, up_ref[...], 1, 1)

    by_half(
        steps,
        lambda: run(up_own, down_own, hid_own, pre_own),
        lambda: run(up_oth, down_oth, hid_oth, pre_oth),
    )

    @pl.when(index == 2 * steps - 1)
    def _():
        finish_rows(
            tiles, lambda at: cot_ref[at].astype(F32), resid_ref, total_ref, gain_ref, out_own, out_oth, attn_ref, mgrad_ref, gain_grad_ref
        )


def join_part(x, mixed, cot, out_pair, gains, up_pair, down_pair, tile=512, chunk=768):
    rows, width = x.shape
    local_ff = up_pair[0].shape[1]
    steps = local_ff // chunk
    shape = jax.ShapeDtypeStruct
    cols = lambda height: [first_cols(height, chunk, steps), second_cols(height, chunk, steps)]
    return pl.pallas_call(
        functools.partial(join_kernel, tile=tile, steps=steps),
        grid=(2 * steps,),
        in_specs=[once(x), once(mixed), once(cot), once(out_pair[0]), once(out_pair[1]), once(gains)] + cols(width) * 2,
        out_specs=[once(x), once(x), whole_shape((8, width))] + cols(rows) * 2,
        out_shape=[shape((rows, width), BF16)] * 2 + [shape((8, width), F32)] + [shape((rows, local_ff), BF16)] * 4,
        scratch_shapes=[
            pltpu.VMEM((rows, width), BF16),
            pltpu.VMEM((rows, width), F32),
            pltpu.VMEM((rows, width), F32),
        ],
        compiler_params=params(48),
        cost_estimate=cost(4 * rows * width * (width + 3 * local_ff), rows * (width * 10 + local_ff * 8) + width * (width + local_ff * 4) * 2, rows * local_ff * 2),
        name="join_part",
    )(x, mixed, cot, *out_pair, gains, *up_pair, *down_pair)


def join_grads_kernel(
    x_ref, mixed_ref, out_own, out_oth, gain_ref, down_own, down_oth, hid_own, hid_oth, pre_own, pre_oth,
    result_ref, up_g_own, up_g_oth, normed_t, sum_ref, *, tile, steps
):
    index = pl.program_id(0)
    width = x_ref.shape[1]
    tiles = row_tiles(x_ref.shape[0], tile)

    @pl.when(index == 0)
    def _():
        @each(tiles)
        def _(at):
            residual = residual_rows(at, x_ref, mixed_ref, out_own, out_oth)
            sum_ref[at] = residual
            normed_t[:, at] = normed_rows(residual, gain_ref[1:2]).T

    def run(down_ref, hid_ref, pre_ref, up_g):
        @each(row_tiles(width, width // 2))
        def _(at):
            up_g[at] = dot(normed_t[at], pre_ref[...], 1, 0).astype(BF16)
        @each(tiles)
        def _(at):
            sum_ref[at] += dot(hid_ref[at], down_ref[...], 1, 1)

    by_half(
        steps,
        lambda: run(down_own, hid_own, pre_own, up_g_own),
        lambda: run(down_oth, hid_oth, pre_oth, up_g_oth),
    )

    @pl.when(index == 2 * steps - 1)
    def _():
        @each(tiles)
        def _(at):
            result_ref[at] = sum_ref[at].astype(BF16)


def join_grads(x, mixed, out_pair, gains, down_pair, hid_pair, pre_pair, tile=512, chunk=512):
    rows, width = x.shape
    local_ff = down_pair[0].shape[1]
    steps = local_ff // chunk
    shape = jax.ShapeDtypeStruct
    cols = lambda height: [first_cols(height, chunk, steps), second_cols(height, chunk, steps)]
    return pl.pallas_call(
        functools.partial(join_grads_kernel, tile=tile, steps=steps),
        grid=(2 * steps,),
        in_specs=[once(x), once(mixed), once(out_pair[0]), once(out_pair[1]), once(gains)] + cols(width) + cols(rows) * 2,
        out_specs=[once(x)] + cols(width),
        out_shape=[shape((rows, width), BF16)] + [shape((width, local_ff), BF16)] * 2,
        scratch_shapes=[
            pltpu.VMEM((width, rows), BF16),
            pltpu.VMEM((rows, width), F32),
        ],
        compiler_params=params(40),
        cost_estimate=cost(2 * rows * width * (width + 6 * local_ff), rows * (width * 8 + local_ff * 8) + width * (width + local_ff * 6) * 2),
        name="join_grads",
    )(x, mixed, *out_pair, gains, *down_pair, *hid_pair, *pre_pair)


def late_kernel(
    x_ref, mixed_ref, cot_ref, spread_ref, out_own, out_oth, gain_ref, up_own, up_oth, down_own, down_oth, slope_own, slope_oth,
    attn_ref, mgrad_ref, gain_grad_ref, up_g_own, up_g_oth,
    normed_t, grad_ref, resid_ref, total_ref, pre_ref, *, tile, steps
):
    index = pl.program_id(0)
    width = x_ref.shape[1]
    tiles = row_tiles(x_ref.shape[0], tile)

    def result_grad(at):
        runs = pl.ds(pl.multiple_of(at.start // RUN, tile // RUN), tile // RUN)
        spread = jnp.broadcast_to(spread_ref[runs][:, None, :], (tile // RUN, RUN, width)).reshape(tile, width)
        return cot_ref[at].astype(F32) + spread

    @pl.when(index == 0)
    def _():
        total_ref[...] = jnp.zeros_like(total_ref)
        @each(tiles)
        def _(at):
            residual = residual_rows(at, x_ref, mixed_ref, out_own, out_oth)
            resid_ref[at] = residual
            normed_t[:, at] = normed_rows(residual, gain_ref[1:2]).T
            grad_ref[at] = result_grad(at).astype(BF16)

    def run(up_ref, down_ref, slope_ref, up_g):
        @each(tiles)
        def _(at):
            pre_low = (dot(grad_ref[at], down_ref[...], 1, 0) * slope_ref[at].astype(F32)).astype(BF16)
            pre_ref[at] = pre_low
            total_ref[at] += dot(pre_low, up_ref[...], 1, 1)
        @each(row_tiles(width, width // 2))
        def _(at):
            up_g[at] = dot(normed_t[at], pre_ref[...], 1, 0).astype(BF16)

    by_half(
        steps,
        lambda: run(up_own, down_own, slope_own, up_g_own),
        lambda: run(up_oth, down_oth, slope_oth, up_g_oth),
    )

    @pl.when(index == 2 * steps - 1)
    def _():
        finish_rows(
            tiles, result_grad, resid_ref, total_ref, gain_ref, out_own, out_oth, attn_ref, mgrad_ref, gain_grad_ref
        )


def late_part(x, mixed, cot, spread, out_pair, gains, up_pair, down_pair, slope_pair, tile=512, chunk=768):
    rows, width = x.shape
    local_ff = up_pair[0].shape[1]
    steps = local_ff // chunk
    shape = jax.ShapeDtypeStruct
    cols = lambda height: [first_cols(height, chunk, steps), second_cols(height, chunk, steps)]
    return pl.pallas_call(
        functools.partial(late_kernel, tile=tile, steps=steps),
        grid=(2 * steps,),
        in_specs=[once(x), once(mixed), once(cot), once(spread), once(out_pair[0]), once(out_pair[1]), once(gains)]
        + cols(width) * 2
        + cols(rows),
        out_specs=[once(x), once(x), whole_shape((8, width))] + cols(width),
        out_shape=[shape((rows, width), BF16)] * 2 + [shape((8, width), F32)] + [shape((width, local_ff), BF16)] * 2,
        scratch_shapes=[
            pltpu.VMEM((width, rows), BF16),
            pltpu.VMEM((rows, width), BF16),
            pltpu.VMEM((rows, width), F32),
            pltpu.VMEM((rows, width), F32),
            pltpu.VMEM((rows, chunk), BF16),
        ],
        compiler_params=params(48),
        cost_estimate=cost(4 * rows * width * (width + 3 * local_ff), rows * (width * 10 + local_ff * 4) + width * (width + local_ff * 6) * 2),
        name="late_part",
    )(x, mixed, cot, spread, *out_pair, gains, *up_pair, *down_pair, *slope_pair)


def blank(*likes):
    return pl.pallas_call(
        lambda *refs: None,
        out_specs=[pl.BlockSpec(memory_space=pl.ANY)] * len(likes),
        out_shape=[jax.ShapeDtypeStruct(shape, dtype) for shape, dtype in likes],
        compiler_params=params(4),
        name="blank",
    )()


def input_kernel(
    x_ref, normed_ref, attn_ref, mixed_ref, d_own, d_oth, w_own, w_oth, gain_ref,
    out_ref, gain_grad_ref, g_own, g_oth, total_ref, normed_t, attn_t, *, tile, steps
):
    index = pl.program_id(0)
    width = x_ref.shape[1]
    half = width // 2
    tiles = row_tiles(x_ref.shape[0], tile)

    @pl.when(index == 0)
    def _():
        total_ref[...] = jnp.zeros_like(total_ref)
        @each(tiles, True)
        def _(at):
            normed_t[:, at] = normed_ref[at].T
            attn_t[:, at] = attn_ref[at].T

    def run(d_ref, w_ref, g_ref):
        @each(tiles, True)
        def _(at):
            total_ref[at] += dot(d_ref[at], w_ref[...], 1, 1)
        @each(row_tiles(width, width // 3), True)
        def _(at):
            g_ref[at] = dot(normed_t[at], d_ref[...], 1, 0).astype(BF16)

    def run_out(cols, g_ref):
        @each(row_tiles(width, width // 3), True)
        def _(at):
            g_ref[at] = dot(attn_t[at], mixed_ref[:, cols], 1, 0).astype(BF16)

    pl.when(index < steps)(lambda: run(d_own, w_own, g_own))
    pl.when(index == steps)(lambda: run_out(slice(0, half), g_own))
    pl.when((index > steps) & (index <= 2 * steps))(lambda: run(d_oth, w_oth, g_oth))

    @pl.when(index == 2 * steps + 1)
    def _():
        run_out(slice(half, width), g_oth)
        gain_grad_ref[...] = jnp.zeros_like(gain_grad_ref)

        @each(tiles, True)
        def _(at):
            part, gain_part = norm_back(x_ref[at].astype(F32), total_ref[at], gain_ref[0:1])
            gain_grad_ref[0:1] += gain_part
            out_ref[at] = (attn_ref[at].astype(F32) + part).astype(BF16)


def input_back(x, normed, attn_low, mixed, d_pair, w_pair, gains, tile=256):
    rows, width = x.shape
    wide = d_pair[0].shape[1]
    chunk = width // 2
    steps = wide // chunk
    shape = jax.ShapeDtypeStruct
    at_own = lambda height: pl.BlockSpec((height, chunk), lambda i: (0, jnp.minimum(i, steps - 1)))
    at_oth = lambda height: pl.BlockSpec((height, chunk), lambda i: (0, jnp.clip(i - steps - 1, 0, steps - 1)))
    return pl.pallas_call(
        functools.partial(input_kernel, tile=tile, steps=steps),
        grid=(2 * steps + 2,),
        in_specs=[once(x), once(x), once(x), once(x), at_own(rows), at_oth(rows), at_own(width), at_oth(width), once(gains)],
        out_specs=[once(x), whole_shape((8, width)), first_cols(width, chunk, steps + 1), second_cols(width, chunk, steps + 1)],
        out_shape=[shape((rows, width), BF16), shape((8, width), F32)] + [shape((width, wide + chunk), BF16)] * 2,
        scratch_shapes=[
            pltpu.VMEM((rows, width), F32),
            pltpu.VMEM((width, rows), BF16),
            pltpu.VMEM((width, rows), BF16),
        ],
        compiler_params=params(32),
        cost_estimate=cost(8 * rows * width * wide + 2 * rows * width * width, rows * (width * 10 + wide * 4) + width * wide * 8),
        name="qkv_back",
    )(x, normed, attn_low, mixed, *d_pair, *w_pair, gains)


def crossed():
    return lax.axis_index("half") != lax.axis_index("mp")


def swap_in(value):
    return lax.ppermute(value, ("half", "mp"), [(1, 2), (2, 1)])


def swapped(value):
    return jnp.where(crossed(), swap_in(value), value)


def from_mate(value):
    return lax.ppermute(value, "half", [(0, 1), (1, 0)])


def along_dp(value, bit):
    return lax.ppermute(value, "dp", [(i, i ^ bit) for i in range(8)])


def pick(value, index, axis=0):
    return lax.dynamic_index_in_dim(value, index, axis, keepdims=False)


def neighbours_swap(value):
    shards, split = lax.axis_size("dp"), lax.axis_size("mp")
    pairs = [
        ((h * shards + d) * split + m, (h * shards + (d ^ 1)) * split + m)
        for h in range(2)
        for d in range(shards)
        for m in range(split)
        if h != m
    ]
    return lax.ppermute(value, ("half", "dp", "mp"), pairs)


def after(value, *others):
    return lax.optimization_barrier((value, *others))[0]


def fetch(weight, gate=None, mate_gate=None):
    received = swap_in(weight if gate is None else after(weight, gate))
    own = jnp.where(crossed(), received if mate_gate is None else after(received, mate_gate), weight)
    return own, from_mate(own), received


def fetch_shared(weight, gate, pass_gate):
    rows, cols = weight.shape
    parts = weight.reshape(2, rows // 2, cols)
    odd = lax.axis_index("dp") % 2
    mine = swap_in(after(pick(parts, odd), gate))
    other = neighbours_swap(after(mine, pass_gate))
    got = jnp.where(odd == 0, jnp.stack([mine, other]), jnp.stack([other, mine]))
    own = jnp.where(crossed(), got, parts).reshape(rows, cols)
    return own, from_mate(own), mine


def low_sum(one, two):
    return (one.astype(F32) + two.astype(F32)).astype(BF16)


def by_place(grad):
    return grad.reshape(2, 2, 2, grad.shape[0] // 8, grad.shape[1])


def pair_summed(part, bit, axis, *gate):
    at = lax.axis_index("dp") // bit % 2
    got = along_dp(after(pick(part, 1 - at, axis), *gate), bit)
    return low_sum(pick(part, at, axis), got)


def x_summed(part, *gate):
    return pair_summed(part, 1, part.ndim - 3, *gate)


def z_summed(part, *gate):
    return pair_summed(pair_summed(part, 2, 1), 4, 0, *gate)


def all_sum(value):
    shards = lax.axis_size("dp")
    if shards != 8:
        return lax.psum(value, ("half", "dp"))
    value = value + from_mate(value)
    for bit in (1, 2, 4):
        value = value + along_dp(value, bit)
    return value


def body(tokens, norm_gains, qkv_w, out_w, up_w, down_w, memory, memory_ids, counts, prefix_mask, cotangent):
    core = lax.axis_index("half")
    layer = lax.axis_index("mp")
    shard_count = lax.axis_size("dp")
    shard_index = lax.axis_index("dp")
    rows, width = tokens.shape[1:]
    questions, k_most = memory_ids.shape
    mem_dev = memory.shape[1]
    score_scale = (4 * width) ** (-0.5)
    local_hd = qkv_w.shape[3]
    padded = 16

    gains = swapped(norm_gains[0])
    x_in = swap_in(tokens[0])
    x = jnp.where(crossed(), x_in, tokens[0])
    *qkv_pair, qkv_in = fetch(qkv_w[0].reshape(width, 3 * local_hd))
    normed, *proj = project(x, gains, qkv_pair)
    *out_pair, _ = fetch(out_w[0], x_in, proj[0])
    *up_pair, up_in = fetch_shared(up_w[0], x_in, proj[0])
    self_mixed = attention(*proj)
    *down_pair, down_in = fetch(down_w[0], qkv_in, self_mixed)
    cot = swapped(after(cotangent[0], down_in))

    slot_total = questions * k_most
    capacity = (slot_total + shard_count - 1) // shard_count
    table = memory[0].reshape(mem_dev, 4 * width)
    local_rows = jnp.concatenate(
        [memory_ids.reshape(-1) % mem_dev, jnp.zeros((capacity * shard_count - slot_total,), jnp.int32)]
    )
    requests = jnp.roll(local_rows.reshape(capacity, shard_count), shard_index, axis=1).T
    asked = lax.all_to_all(requests, "dp", split_axis=0, concat_axis=0, tiled=True).reshape(-1)
    answer = dot((asked[:, None] == jnp.arange(mem_dev)[None, :]).astype(BF16), table, 1, 0).astype(BF16)
    answers = lax.all_to_all(answer, "dp", split_axis=0, concat_axis=0, tiled=True)
    answers = swapped(after(answers, up_in))
    at = jnp.arange(questions * padded)
    slot = at % padded
    flat = at // padded * k_most + slot
    source = (shard_index + flat % shard_count) % shard_count * capacity + flat // shard_count
    source = jnp.where(slot < k_most, source, -1)
    chosen = (source[:, None] == jnp.arange(capacity * shard_count)[None, :]).astype(BF16)
    found = dot(chosen, answers, 1, 0).astype(BF16)
    half = width // 2
    other_way = jnp.concatenate(
        [found[:, c * width + h * half : c * width + (h + 1) * half] for c in range(4) for h in (1, 0)], axis=1
    )
    found_heads = jnp.where(core == 0, found, other_way).reshape(questions, padded, 4 * width)
    found = found.reshape(questions, padded, 4 * width)

    valid = (jnp.arange(k_most)[None, :] < counts[:, None])[:, None, :] & (
        jnp.swapaxes(prefix_mask.reshape(questions, k_most, 2), 1, 2) == 1
    )
    valid = jnp.pad(valid.astype(F32), ((0, 0), (0, 0), (0, padded - k_most))).reshape(questions, 2 * padded)
    valid = (swapped(valid) > 0.5) & (layer == 1)

    def biases(scores):
        wide = jnp.tile(jnp.pad(scores.astype(F32), ((0, 0), (0, padded - k_most))), (1, 2))
        bias = jnp.where(valid, wide, MASKED)
        return jnp.broadcast_to(bias[:, :, None], (questions, 2 * padded, LANES))

    joining = layer == 1
    pooled = pooled_result(x, self_mixed, out_pair, gains, up_pair, down_pair)
    pooled = (pooled * (1.0 / RUN)).reshape(questions, 4 * width)
    scores = jnp.sum(pooled[:, None, :] * found[:, :k_most].astype(F32), axis=-1) * score_scale
    sent = lax.ppermute(scores.astype(BF16), "mp", [(0, 1)])

    bias = biases(sent)
    local_ff = up_w.shape[2]
    tall = ((rows, local_ff), BF16)
    flat = ((rows, width), BF16)
    grad_like = ((width, local_ff), BF16)
    run_like = ((rows // RUN, local_ff), BF16)
    slot_like = ((questions, 2 * padded, LANES), F32)
    gain_like = ((8, width), F32)

    def join_first():
        mixed = attention(*proj, (found_heads, bias))
        attn_low, mgrad, gain_two, hid_own, hid_oth, pre_own, pre_oth = join_part(
            x, mixed, cot, out_pair, gains, up_pair, down_pair
        )
        slots = slot_sums(*proj, found_heads, bias, mgrad)
        unused = blank(grad_like, grad_like, run_like, run_like)
        return mixed, attn_low, mgrad, gain_two, hid_own, hid_oth, pre_own, pre_oth, slots, *unused

    def key_first():
        result, slope_own, slope_oth, *rest = early_part(x, self_mixed, cot, out_pair, gains, up_pair, down_pair)
        mgrad, gain_two, pre_own, pre_oth, slots = blank(flat, gain_like, tall, tall, slot_like)
        return self_mixed, result, mgrad, gain_two, slope_own, slope_oth, pre_own, pre_oth, slots, *rest

    (mixed, flat_one, mgrad, gain_two, tall_own, tall_oth, pre_own, pre_oth, slots, *key_down, run_own, run_oth) = lax.cond(
        joining, join_first, key_first
    )
    slot_grad = slots[:, :, 0]
    score_low = (slot_grad[:, :k_most] + slot_grad[:, padded : padded + k_most]).astype(BF16)
    score_in = lax.ppermute(score_low, "mp", [(1, 0)])

    scale = score_scale / RUN
    spread = jnp.sum(
        (score_in.astype(F32) * scale)[:, :, None] * found[:, :k_most].astype(F32), axis=1
    ).reshape(rows // RUN, width)

    def weight_grad(rows_of, cols_of, base=0.0):
        return (dot(rows_of, cols_of, 0, 0) + base).astype(BF16)

    def join_down():
        return weight_grad(cot, tall_own), weight_grad(cot, tall_oth)

    def key_down_all():
        spread_low = spread.astype(BF16)
        return tuple(
            weight_grad(spread_low, r, g.astype(F32)) for g, r in zip(key_down, (run_own, run_oth))
        )

    down_own, down_oth = lax.cond(joining, join_down, key_down_all)
    down_grad = low_sum(down_own, from_mate(down_oth))

    def join_second():
        result, up_own, up_oth = join_grads(
            x, mixed, out_pair, gains, down_pair, (tall_own, tall_oth), (pre_own, pre_oth)
        )
        return result, flat_one, mgrad, gain_two, up_own, up_oth

    def key_second():
        return flat_one, *late_part(
            x, mixed, cot, spread, out_pair, gains, up_pair, down_pair, (tall_own, tall_oth)
        )

    result, attn_low, mgrad, gain_two, up_own, up_oth = lax.cond(joining, join_second, key_second)
    ring = shard_count == 8
    down_part = x_summed(by_place(down_grad)) if ring else down_grad
    up_grad = low_sum(up_own, from_mate(after(up_oth, down_part)))
    d_own, d_oth, _ = attention_back(*proj, found_heads, bias, mgrad)
    result_in = swap_in(result)
    down_near = far = ()
    if ring:
        up_part = x_summed(by_place(up_grad), result_in)
        down_near = (pair_summed(down_part, 2, 1),)
        far = (pair_summed(down_near[0], 4, 0), up_part)
    grad_in, gain_one, head_own, head_oth = input_back(
        x, normed, attn_low, mixed, (after(d_own, up_grad, *down_near), d_oth), qkv_pair, gains
    )
    grad_in_recv = swap_in(grad_in)
    small = all_sum(after(jnp.concatenate([gain_one[:1], gain_two[:1]], axis=0), *far))
    head_grad = low_sum(head_own, after(from_mate(after(head_oth, *far)), small))

    def placed(sum_rows):
        return swapped(sum_rows.astype(BF16)).astype(F32)

    if ring:
        first, second = jnp.split(by_place(head_grad), 2, axis=-1)
        second = pair_summed(second, 2, 1)
        first = x_summed(first)
        up_near = pair_summed(up_part, 2, 1, second)
        second = pair_summed(second, 4, 0)
        down_g, up_g = placed(after(far[0], second)), placed(pair_summed(up_near, 4, 0))
        head_g = placed(jnp.concatenate([z_summed(first), x_summed(second)], axis=-1))
    else:
        down_g, up_g, head_g = (
            placed(lax.psum_scatter(g.astype(F32), "dp", scatter_dimension=0, tiled=True))
            for g in (down_part, up_grad, head_grad)
        )
    score_out = jnp.where(joining, score_low, score_in).astype(F32)
    score_out = jnp.pad(score_out.reshape(-1), (0, width - slot_total))[None]
    small = swapped(after(jnp.concatenate([small, score_out]), grad_in_recv, second if ring else head_grad))
    gain_grads, score_out = small[:2], small[2, :slot_total].reshape(questions, k_most)
    activations = jnp.where(crossed(), result_in, result)
    input_grad = jnp.where(crossed(), after(grad_in_recv, first) if ring else grad_in_recv, grad_in).astype(F32)
    return (
        activations[None],
        input_grad[None],
        score_out,
        gain_grads[None],
        head_g[:, : 3 * local_hd].reshape(1, -1, 3, local_hd),
        head_g[None, :, 3 * local_hd :],
        up_g[None],
        down_g[None],
    )


def solution(mesh):
    placed = (
        P("half", ("dp", "mp"), None),
        P("half", None, None),
        P("half", None, None, "mp"),
        P("half", None, "mp"),
        P("half", None, "mp"),
        P("half", None, "mp"),
        P("half", "dp", None, None),
        P(("dp", "mp"), None),
        P(("dp", "mp")),
        P(("dp", "mp"), None),
        P("half", ("dp", "mp"), None),
    )
    return jax.shard_map(
        body,
        mesh=mesh,
        in_specs=placed,
        out_specs=(
            P("half", ("dp", "mp"), None),
            P("half", ("dp", "mp"), None),
            P(("dp", "mp"), None),
            P("half", None, None),
            P("half", "dp", None, "mp"),
            P("half", "dp", "mp"),
            P("half", "dp", "mp"),
            P("half", "dp", "mp"),
        ),
        check_vma=False,
    )
```

```python
import functools

import jax
import jax.numpy as jnp
from jax import lax
from jax.experimental import pallas as pl
from jax.experimental.pallas import tpu as pltpu
from jax.sharding import PartitionSpec as P

HDIM = 64
QLEN = 64
RUN = 16
LANES = 128
NORM_EPS = 1e-06
MASKED = -1e30
F32 = jnp.float32
BF16 = jnp.bfloat16
GELU_A = 0.7978845608028654
GELU_B = 0.044715 * GELU_A


def dot(a, b, ca, cb):
    return lax.dot_general(a, b, (((ca,), (cb,)), ((), ())), preferred_element_type=F32)


def params(mebibytes):
    return pltpu.CompilerParams(vmem_limit_bytes=mebibytes << 20)


def cost(flops, nbytes, trans=0):
    return pl.CostEstimate(flops=int(flops), bytes_accessed=int(nbytes), transcendentals=int(trans))


def head_stack(block):
    lane = lax.broadcasted_iota(jnp.int32, block.shape, 1)
    zero = jnp.zeros_like(block)
    return jnp.concatenate(
        [jnp.where(lane < HDIM, block, zero), jnp.where(lane < HDIM, zero, block)], axis=0
    )


def head_merge(stacked):
    lane = lax.broadcasted_iota(jnp.int32, (QLEN, LANES), 1)
    return jnp.where(lane < HDIM, stacked[:QLEN], stacked[QLEN:])


def pair_views(own_ref, oth_ref, found_ref, question, pair, local_hd, width):
    ref = own_ref if pair * LANES < local_hd else oth_ref
    base = pair * LANES % local_hd
    rows = slice(question * QLEN, (question + 1) * QLEN)
    query = ref[rows, base : base + LANES]
    key = ref[rows, local_hd + base : local_hd + base + LANES]
    value = ref[rows, 2 * local_hd + base : 2 * local_hd + base + LANES]
    stack = head_stack(query * jnp.asarray(HDIM**-0.5, BF16))
    if found_ref is None:
        return stack, key, value
    col = pair * LANES
    pref = [found_ref[question, :, c * width + col : c * width + col + LANES] for c in range(4)]
    keys = jnp.concatenate([key, pref[0], pref[1]], axis=0)
    values = jnp.concatenate([value, pref[2], pref[3]], axis=0)
    return stack, keys, values


def pair_logits(stack, keys, bias):
    logits = dot(keys, stack, 1, 1)
    if bias is None:
        return logits
    return jnp.concatenate([logits[:QLEN], logits[QLEN:] + bias], axis=0)


def softmax_down(logits):
    weights = jnp.exp(logits - jnp.max(logits, axis=0, keepdims=True))
    return weights * (1.0 / jnp.sum(weights, axis=0, keepdims=True))


def grouped(questions, pairs, group):
    items = [(question, pair) for question in range(questions) for pair in range(pairs)]
    return [items[at : at + group] for at in range(0, len(items), group)]


def attention_kernel(own_ref, oth_ref, *refs, questions, local_hd, width, group):
    found_ref, bias_ref, mixed_ref = refs if len(refs) == 3 else (None, None, *refs)
    for items in grouped(questions, width // LANES, group):
        views = [pair_views(own_ref, oth_ref, found_ref, q, p, local_hd, width) for q, p in items]
        logits = [pair_logits(v[0], v[1], None if bias_ref is None else bias_ref[q]) for v, (q, p) in zip(views, items)]
        probs = [softmax_down(l).astype(BF16) for l in logits]
        mixed = [dot(p, v[2], 0, 0) for p, v in zip(probs, views)]
        for m, (q, p) in zip(mixed, items):
            mixed_ref[q * QLEN : (q + 1) * QLEN, p * LANES : (p + 1) * LANES] = head_merge(m).astype(BF16)


def attention(own, oth, prefix=(), questions=4, group=12):
    rows, local_hd = own.shape[0], own.shape[1] // 3
    width = 2 * local_hd
    count = rows // QLEN
    block = questions * QLEN
    return pl.pallas_call(
        functools.partial(attention_kernel, questions=questions, local_hd=local_hd, width=width, group=group),
        grid=(count // questions,),
        in_specs=[pl.BlockSpec((block, 3 * local_hd), lambda i: (i, 0))] * 2
        + [pl.BlockSpec((questions, *a.shape[1:]), lambda i: (i, 0, 0)) for a in prefix],
        out_specs=pl.BlockSpec((block, width), lambda i: (i, 0)),
        out_shape=jax.ShapeDtypeStruct((rows, width), BF16),
        compiler_params=params(20),
        cost_estimate=cost(rows * width * 96 * 8, rows * width * 8, rows * 12 * 96),
        name="attend",
    )(own, oth, *prefix)


def attention_back_kernel(
    own_ref, oth_ref, found_ref, bias_ref, mixed_ref, down_ref, doth_ref, slot_ref, *, questions, local_hd, width, group
):
    totals = [None] * questions
    for items in grouped(questions, width // LANES, group):
        views = [pair_views(own_ref, oth_ref, found_ref, q, p, local_hd, width) for q, p in items]
        logits = [pair_logits(v[0], v[1], bias_ref[q]) for v, (q, p) in zip(views, items)]
        grads = [
            head_stack(mixed_ref[q * QLEN : (q + 1) * QLEN, p * LANES : (p + 1) * LANES]) for q, p in items
        ]
        prob_grads = [dot(v[2], g, 1, 1) for v, g in zip(views, grads)]
        probs = [softmax_down(l) for l in logits]
        deltas = [jnp.sum(p * g, axis=0, keepdims=True) for p, g in zip(probs, prob_grads)]
        logit_grads = [p * (g - d) for p, g, d in zip(probs, prob_grads, deltas)]
        lows = [l.astype(BF16) for l in logit_grads]
        value_grads = [dot(p[:QLEN].astype(BF16), g, 1, 0) for p, g in zip(probs, grads)]
        key_grads = [dot(l[:QLEN], v[0], 1, 0) for l, v in zip(lows, views)]
        query_grads = [dot(l, v[1], 0, 0) for l, v in zip(lows, views)]
        for at, (q, p) in enumerate(items):
            part = logit_grads[at][QLEN:]
            totals[q] = part if totals[q] is None else totals[q] + part
            out = down_ref if p * LANES < local_hd else doth_ref
            base = p * LANES % local_hd
            rows = slice(q * QLEN, (q + 1) * QLEN)
            out[rows, base : base + LANES] = (head_merge(query_grads[at]) * HDIM**-0.5).astype(BF16)
            out[rows, local_hd + base : local_hd + base + LANES] = key_grads[at].astype(BF16)
            out[rows, 2 * local_hd + base : 2 * local_hd + base + LANES] = value_grads[at].astype(BF16)
    for q in range(questions):
        slot_ref[q] = jnp.broadcast_to(jnp.sum(totals[q], axis=1, keepdims=True), totals[q].shape)


def attention_back(own, oth, found, bias, mixed_low, questions=2, group=12):
    rows, local_hd = own.shape[0], own.shape[1] // 3
    width = 2 * local_hd
    count = rows // QLEN
    slots = found.shape[1]
    block = questions * QLEN
    wide = pl.BlockSpec((block, 3 * local_hd), lambda i: (i, 0))
    bias_spec = pl.BlockSpec((questions, 2 * slots, LANES), lambda i: (i, 0, 0))
    return pl.pallas_call(
        functools.partial(
            attention_back_kernel, questions=questions, local_hd=local_hd, width=width, group=group
        ),
        grid=(count // questions,),
        in_specs=[
            wide,
            wide,
            pl.BlockSpec((questions, slots, 4 * width), lambda i: (i, 0, 0)),
            bias_spec,
            pl.BlockSpec((block, width), lambda i: (i, 0)),
        ],
        out_specs=[wide, wide, bias_spec],
        out_shape=[
            jax.ShapeDtypeStruct((rows, 3 * local_hd), BF16),
            jax.ShapeDtypeStruct((rows, 3 * local_hd), BF16),
            jax.ShapeDtypeStruct((count, 2 * slots, LANES), F32),
        ],
        compiler_params=params(24),
        cost_estimate=cost(rows * width * 96 * 20, rows * width * 16, rows * 12 * 96),
        name="attend_back",
    )(own, oth, found, bias, mixed_low)


def slot_kernel(own_ref, oth_ref, found_ref, bias_ref, mixed_ref, slot_ref, *, questions, local_hd, width, group):
    totals = [None] * questions
    for items in grouped(questions, width // LANES, group):
        views = [pair_views(own_ref, oth_ref, found_ref, q, p, local_hd, width) for q, p in items]
        logits = [pair_logits(v[0], v[1], bias_ref[q]) for v, (q, p) in zip(views, items)]
        grads = [
            head_stack(mixed_ref[q * QLEN : (q + 1) * QLEN, p * LANES : (p + 1) * LANES]) for q, p in items
        ]
        prob_grads = [dot(v[2], g, 1, 1) for v, g in zip(views, grads)]
        probs = [softmax_down(l) for l in logits]
        deltas = [jnp.sum(p * g, axis=0, keepdims=True) for p, g in zip(probs, prob_grads)]
        parts = [p[QLEN:] * (g[QLEN:] - d) for p, g, d in zip(probs, prob_grads, deltas)]
        for part, (q, p) in zip(parts, items):
            totals[q] = part if totals[q] is None else totals[q] + part
    for q in range(questions):
        slot_ref[q] = jnp.broadcast_to(jnp.sum(totals[q], axis=1, keepdims=True), totals[q].shape)


def slot_sums(own, oth, found, bias, mixed_low, questions=4, group=12):
    rows, local_hd = own.shape[0], own.shape[1] // 3
    width = 2 * local_hd
    count = rows // QLEN
    slots = found.shape[1]
    block = questions * QLEN
    wide = pl.BlockSpec((block, 3 * local_hd), lambda i: (i, 0))
    bias_spec = pl.BlockSpec((questions, 2 * slots, LANES), lambda i: (i, 0, 0))
    return pl.pallas_call(
        functools.partial(slot_kernel, questions=questions, local_hd=local_hd, width=width, group=group),
        grid=(count // questions,),
        in_specs=[
            wide,
            wide,
            pl.BlockSpec((questions, slots, 4 * width), lambda i: (i, 0, 0)),
            bias_spec,
            pl.BlockSpec((block, width), lambda i: (i, 0)),
        ],
        out_specs=bias_spec,
        out_shape=jax.ShapeDtypeStruct((count, 2 * slots, LANES), F32),
        compiler_params=params(20),
        cost_estimate=cost(rows * width * 96 * 8, rows * width * 12, rows * 12 * 96),
        name="slot_sums",
    )(own, oth, found, bias, mixed_low)


def rms_scale(block):
    return lax.rsqrt(jnp.mean(block * block, axis=-1, keepdims=True) + NORM_EPS)


def row_tiles(rows, tile):
    return rows, tile


def each(tiles, unrolled=False):
    rows, tile = tiles

    def loop(body):
        if unrolled:
            for at in range(0, rows, tile):
                body(slice(at, at + tile))
            return

        @pl.loop(0, rows // tile)
        def _(step):
            body(pl.ds(pl.multiple_of(step * tile, tile), tile))

    return loop


def whole(array):
    return pl.BlockSpec(array.shape, lambda i: (0,) * array.ndim)


def whole_shape(shape):
    return pl.BlockSpec(shape, lambda i: (0, 0))


def first_cols(rows, chunk, steps):
    return pl.BlockSpec((rows, chunk), lambda i: (0, jnp.minimum(i, steps - 1)))


def second_cols(rows, chunk, steps):
    return pl.BlockSpec((rows, chunk), lambda i: (0, jnp.maximum(i - steps, 0)))


def by_half(steps, first, second):
    index = pl.program_id(0)
    pl.when(index < steps)(first)
    pl.when(index >= steps)(second)


def project_kernel(x_ref, gain_ref, w_own, w_oth, normed_ref, own_ref, oth_ref, *, tile, steps):
    tiles = row_tiles(x_ref.shape[0], tile)

    @pl.when(pl.program_id(0) == 0)
    def _():
        @each(tiles, True)
        def _(at):
            block = x_ref[at].astype(F32)
            normed_ref[at] = (block * rms_scale(block) * gain_ref[0:1]).astype(BF16)

    def run(w_ref, out_ref):
        @each(tiles, True)
        def _(at):
            out_ref[at] = dot(normed_ref[at], w_ref[...], 1, 0).astype(BF16)

    by_half(steps, lambda: run(w_own, own_ref), lambda: run(w_oth, oth_ref))


def project(x, gains, w_pair, tile=256, chunk=384):
    rows, width = x.shape
    cols = w_pair[0].shape[1]
    steps = cols // chunk
    shape = jax.ShapeDtypeStruct
    return pl.pallas_call(
        functools.partial(project_kernel, tile=tile, steps=steps),
        grid=(2 * steps,),
        in_specs=[whole(x), whole(gains), first_cols(width, chunk, steps), second_cols(width, chunk, steps)],
        out_specs=[whole(x), first_cols(rows, chunk, steps), second_cols(rows, chunk, steps)],
        out_shape=[shape((rows, width), BF16), shape((rows, cols), BF16), shape((rows, cols), BF16)],
        compiler_params=params(24),
        cost_estimate=cost(4 * rows * width * cols, rows * (width + cols) * 4 + width * cols * 4),
        name="project",
    )(x, gains, *w_pair)


def norm_back(block, grad, gain):
    scale = rms_scale(block)
    weighted = grad * gain
    inner = jnp.mean(block * weighted, axis=-1, keepdims=True)
    return (
        scale * weighted - block * (scale * scale * scale * inner),
        jnp.sum(grad * block * scale, axis=0, keepdims=True),
    )


def gelu_terms(pre):
    cube = GELU_B * (pre * pre)
    return cube, jnp.tanh(pre * (GELU_A + cube)), 0.5 * pre


def gelu_value(terms):
    _, bend, half_pre = terms
    return half_pre * bend + half_pre


def gelu_slope(terms):
    cube, bend, half_pre = terms
    return (0.5 + 0.5 * bend) + half_pre * (1.0 - bend * bend) * (GELU_A + 3.0 * cube)


def residual_rows(at, x_ref, mixed_ref, out_own, out_oth):
    half = mixed_ref.shape[1] // 2
    return (
        x_ref[at].astype(F32)
        + dot(mixed_ref[at, :half], out_own[...], 1, 1)
        + dot(mixed_ref[at, half:], out_oth[...], 1, 1)
    )


def normed_rows(residual, gain):
    return (residual * rms_scale(residual) * gain).astype(BF16)


def score_kernel(
    x_ref, mixed_ref, out_own, out_oth, gain_ref, up_own, up_oth, down_own, down_oth,
    pooled_ref, normed_ref, total_ref, *, tile, steps
):
    index = pl.program_id(0)
    tiles = row_tiles(x_ref.shape[0], tile)

    @pl.when(index == 0)
    def _():
        @each(tiles, True)
        def _(at):
            residual = residual_rows(at, x_ref, mixed_ref, out_own, out_oth)
            total_ref[at] = residual
            normed_ref[at] = normed_rows(residual, gain_ref[1:2])

    def run(up_ref, down_ref):
        @each(tiles, True)
        def _(at):
            hidden = gelu_value(gelu_terms(dot(normed_ref[at], up_ref[...], 1, 0))).astype(BF16)
            total_ref[at] += dot(hidden, down_ref[...], 1, 1)

    by_half(steps, lambda: run(up_own, down_own), lambda: run(up_oth, down_oth))

    @pl.when(index == 2 * steps - 1)
    def _():
        @each(tiles, True)
        def _(at):
            result = total_ref[at]
            runs = slice(at.start // RUN, at.stop // RUN)
            pooled_ref[runs] = jnp.sum(result.reshape(tile // RUN, RUN, result.shape[1]), axis=1)


def once(array):
    return pl.BlockSpec(array.shape, lambda i: (0,) * array.ndim, pipeline_mode=pl.Buffered(1))


def pooled_result(x, mixed, out_pair, gains, up_pair, down_pair, tile=256, chunk=768):
    rows, width = x.shape
    local_ff = up_pair[0].shape[1]
    steps = local_ff // chunk
    cols = [first_cols(width, chunk, steps), second_cols(width, chunk, steps)]
    return pl.pallas_call(
        functools.partial(score_kernel, tile=tile, steps=steps),
        grid=(2 * steps,),
        in_specs=[once(x), once(mixed), once(out_pair[0]), once(out_pair[1]), once(gains)] + cols * 2,
        out_specs=whole_shape((rows // RUN, width)),
        out_shape=jax.ShapeDtypeStruct((rows // RUN, width), F32),
        scratch_shapes=[pltpu.VMEM((rows, width), BF16), pltpu.VMEM((rows, width), F32)],
        compiler_params=params(30),
        cost_estimate=cost(2 * rows * width * (width + 4 * local_ff), rows * width * 4 + width * (width + local_ff * 4) * 2, rows * local_ff * 2),
        name="pooled_result",
    )(x, mixed, *out_pair, gains, *up_pair, *down_pair)


def early_kernel(
    x_ref, mixed_ref, cot_ref, out_own, out_oth, gain_ref, up_own, up_oth, down_own, down_oth,
    result_ref, slope_own, slope_oth, grad_own, grad_oth, run_own, run_oth,
    normed_ref, sum_ref, left_ref, hid_ref, *, tile, steps
):
    index = pl.program_id(0)
    rows, width = x_ref.shape
    runs = rows // RUN
    tiles = row_tiles(rows, tile)

    @pl.when(index == 0)
    def _():
        @each(tiles)
        def _(at):
            residual = residual_rows(at, x_ref, mixed_ref, out_own, out_oth)
            sum_ref[at] = residual
            normed_ref[at] = normed_rows(residual, gain_ref[1:2])
            left_ref[:width, at] = cot_ref[at].T
        run_of = lax.broadcasted_iota(jnp.int32, (runs, rows), 0) * RUN
        row_at = lax.broadcasted_iota(jnp.int32, (runs, rows), 1)
        left_ref[width:] = jnp.where((row_at >= run_of) & (row_at < run_of + RUN), 1.0, 0.0).astype(BF16)

    def run(up_ref, down_ref, slope_ref, grad_ref, run_ref):
        @each(tiles)
        def _(at):
            terms = gelu_terms(dot(normed_ref[at], up_ref[...], 1, 0))
            hidden = gelu_value(terms).astype(BF16)
            hid_ref[at] = hidden
            slope_ref[at] = gelu_slope(terms).astype(BF16)
            sum_ref[at] += dot(hidden, down_ref[...], 1, 1)
        @each(row_tiles(width, width // 2))
        def _(at):
            grad_ref[at] = dot(left_ref[at], hid_ref[...], 1, 0).astype(BF16)
        run_ref[...] = dot(left_ref[width:], hid_ref[...], 1, 0).astype(BF16)

    by_half(
        steps,
        lambda: run(up_own, down_own, slope_own, grad_own, run_own),
        lambda: run(up_oth, down_oth, slope_oth, grad_oth, run_oth),
    )

    @pl.when(index == 2 * steps - 1)
    def _():
        @each(tiles)
        def _(at):
            result_ref[at] = sum_ref[at].astype(BF16)


def early_part(x, mixed, cot, out_pair, gains, up_pair, down_pair, tile=512, chunk=512):
    rows, width = x.shape
    local_ff = up_pair[0].shape[1]
    runs = rows // RUN
    steps = local_ff // chunk
    shape = jax.ShapeDtypeStruct
    cols = lambda height: [first_cols(height, chunk, steps), second_cols(height, chunk, steps)]
    return pl.pallas_call(
        functools.partial(early_kernel, tile=tile, steps=steps),
        grid=(2 * steps,),
        in_specs=[once(x), once(mixed), once(cot), once(out_pair[0]), once(out_pair[1]), once(gains)] + cols(width) * 2,
        out_specs=[once(x)] + cols(rows) + cols(width) + cols(runs),
        out_shape=[shape((rows, width), BF16)]
        + [shape((rows, local_ff), BF16)] * 2
        + [shape((width, local_ff), BF16)] * 2
        + [shape((runs, local_ff), BF16)] * 2,
        scratch_shapes=[
            pltpu.VMEM((rows, width), BF16),
            pltpu.VMEM((rows, width), F32),
            pltpu.VMEM((width + runs, rows), BF16),
            pltpu.VMEM((rows, chunk), BF16),
        ],
        compiler_params=params(40),
        cost_estimate=cost(2 * rows * width * (width + 6 * local_ff), rows * (width * 8 + local_ff * 4) + width * (width + local_ff * 6) * 2, rows * local_ff * 2),
        name="early_part",
    )(x, mixed, cot, *out_pair, gains, *up_pair, *down_pair)


def finish_rows(tiles, grad_of, resid_ref, total_ref, gain_ref, out_own, out_oth, attn_ref, mgrad_ref, gain_grad_ref):
    half = out_own.shape[1]
    gain_grad_ref[...] = jnp.zeros_like(gain_grad_ref)

    @each(tiles)
    def _(at):
        part, gain_part = norm_back(resid_ref[at], total_ref[at], gain_ref[1:2])
        gain_grad_ref[0:1] += gain_part
        attn_low = (grad_of(at) + part).astype(BF16)
        attn_ref[at] = attn_low
        mgrad_ref[at, :half] = dot(attn_low, out_own[...], 1, 0).astype(BF16)
        mgrad_ref[at, half:] = dot(attn_low, out_oth[...], 1, 0).astype(BF16)


def join_kernel(
    x_ref, mixed_ref, cot_ref, out_own, out_oth, gain_ref, up_own, up_oth, down_own, down_oth,
    attn_ref, mgrad_ref, gain_grad_ref, hid_own, hid_oth, pre_own, pre_oth,
    normed_ref, resid_ref, total_ref, *, tile, steps
):
    index = pl.program_id(0)
    tiles = row_tiles(x_ref.shape[0], tile)

    @pl.when(index == 0)
    def _():
        total_ref[...] = jnp.zeros_like(total_ref)
        @each(tiles, True)
        def _(at):
            residual = residual_rows(at, x_ref, mixed_ref, out_own, out_oth)
            resid_ref[at] = residual
            normed_ref[at] = normed_rows(residual, gain_ref[1:2])

    def run(up_ref, down_ref, hid_ref, pre_ref):
        @each(tiles, True)
        def _(at):
            terms = gelu_terms(dot(normed_ref[at], up_ref[...], 1, 0))
            hid_ref[at] = gelu_value(terms).astype(BF16)
            pre_low = (dot(cot_ref[at], down_ref[...], 1, 0) * gelu_slope(terms)).astype(BF16)
            pre_ref[at] = pre_low
            total_ref[at] += dot(pre_low, up_ref[...], 1, 1)

    by_half(
        steps,
        lambda: run(up_own, down_own, hid_own, pre_own),
        lambda: run(up_oth, down_oth, hid_oth, pre_oth),
    )

    @pl.when(index == 2 * steps - 1)
    def _():
        finish_rows(
            tiles, lambda at: cot_ref[at].astype(F32), resid_ref, total_ref, gain_ref, out_own, out_oth, attn_ref, mgrad_ref, gain_grad_ref
        )


def join_part(x, mixed, cot, out_pair, gains, up_pair, down_pair, tile=512, chunk=768):
    rows, width = x.shape
    local_ff = up_pair[0].shape[1]
    steps = local_ff // chunk
    shape = jax.ShapeDtypeStruct
    cols = lambda height: [first_cols(height, chunk, steps), second_cols(height, chunk, steps)]
    return pl.pallas_call(
        functools.partial(join_kernel, tile=tile, steps=steps),
        grid=(2 * steps,),
        in_specs=[once(x), once(mixed), once(cot), once(out_pair[0]), once(out_pair[1]), once(gains)] + cols(width) * 2,
        out_specs=[once(x), once(x), whole_shape((8, width))] + cols(rows) * 2,
        out_shape=[shape((rows, width), BF16)] * 2 + [shape((8, width), F32)] + [shape((rows, local_ff), BF16)] * 4,
        scratch_shapes=[
            pltpu.VMEM((rows, width), BF16),
            pltpu.VMEM((rows, width), F32),
            pltpu.VMEM((rows, width), F32),
        ],
        compiler_params=params(48),
        cost_estimate=cost(4 * rows * width * (width + 3 * local_ff), rows * (width * 10 + local_ff * 8) + width * (width + local_ff * 4) * 2, rows * local_ff * 2),
        name="join_part",
    )(x, mixed, cot, *out_pair, gains, *up_pair, *down_pair)


def join_grads_kernel(
    x_ref, mixed_ref, out_own, out_oth, gain_ref, down_own, down_oth, hid_own, hid_oth, pre_own, pre_oth,
    result_ref, up_g_own, up_g_oth, normed_t, sum_ref, *, tile, steps
):
    index = pl.program_id(0)
    width = x_ref.shape[1]
    tiles = row_tiles(x_ref.shape[0], tile)

    @pl.when(index == 0)
    def _():
        @each(tiles)
        def _(at):
            residual = residual_rows(at, x_ref, mixed_ref, out_own, out_oth)
            sum_ref[at] = residual
            normed_t[:, at] = normed_rows(residual, gain_ref[1:2]).T

    def run(down_ref, hid_ref, pre_ref, up_g):
        @each(row_tiles(width, width // 2))
        def _(at):
            up_g[at] = dot(normed_t[at], pre_ref[...], 1, 0).astype(BF16)
        @each(tiles)
        def _(at):
            sum_ref[at] += dot(hid_ref[at], down_ref[...], 1, 1)

    by_half(
        steps,
        lambda: run(down_own, hid_own, pre_own, up_g_own),
        lambda: run(down_oth, hid_oth, pre_oth, up_g_oth),
    )

    @pl.when(index == 2 * steps - 1)
    def _():
        @each(tiles)
        def _(at):
            result_ref[at] = sum_ref[at].astype(BF16)


def join_grads(x, mixed, out_pair, gains, down_pair, hid_pair, pre_pair, tile=512, chunk=512):
    rows, width = x.shape
    local_ff = down_pair[0].shape[1]
    steps = local_ff // chunk
    shape = jax.ShapeDtypeStruct
    cols = lambda height: [first_cols(height, chunk, steps), second_cols(height, chunk, steps)]
    return pl.pallas_call(
        functools.partial(join_grads_kernel, tile=tile, steps=steps),
        grid=(2 * steps,),
        in_specs=[once(x), once(mixed), once(out_pair[0]), once(out_pair[1]), once(gains)] + cols(width) + cols(rows) * 2,
        out_specs=[once(x)] + cols(width),
        out_shape=[shape((rows, width), BF16)] + [shape((width, local_ff), BF16)] * 2,
        scratch_shapes=[
            pltpu.VMEM((width, rows), BF16),
            pltpu.VMEM((rows, width), F32),
        ],
        compiler_params=params(40),
        cost_estimate=cost(2 * rows * width * (width + 6 * local_ff), rows * (width * 8 + local_ff * 8) + width * (width + local_ff * 6) * 2),
        name="join_grads",
    )(x, mixed, *out_pair, gains, *down_pair, *hid_pair, *pre_pair)


def late_kernel(
    x_ref, mixed_ref, cot_ref, spread_ref, out_own, out_oth, gain_ref, up_own, up_oth, down_own, down_oth, slope_own, slope_oth,
    attn_ref, mgrad_ref, gain_grad_ref, up_g_own, up_g_oth,
    normed_t, grad_ref, resid_ref, total_ref, pre_ref, *, tile, steps
):
    index = pl.program_id(0)
    width = x_ref.shape[1]
    tiles = row_tiles(x_ref.shape[0], tile)

    def result_grad(at):
        runs = pl.ds(pl.multiple_of(at.start // RUN, tile // RUN), tile // RUN)
        spread = jnp.broadcast_to(spread_ref[runs][:, None, :], (tile // RUN, RUN, width)).reshape(tile, width)
        return cot_ref[at].astype(F32) + spread

    @pl.when(index == 0)
    def _():
        total_ref[...] = jnp.zeros_like(total_ref)
        @each(tiles)
        def _(at):
            residual = residual_rows(at, x_ref, mixed_ref, out_own, out_oth)
            resid_ref[at] = residual
            normed_t[:, at] = normed_rows(residual, gain_ref[1:2]).T
            grad_ref[at] = result_grad(at).astype(BF16)

    def run(up_ref, down_ref, slope_ref, up_g):
        @each(tiles)
        def _(at):
            pre_low = (dot(grad_ref[at], down_ref[...], 1, 0) * slope_ref[at].astype(F32)).astype(BF16)
            pre_ref[at] = pre_low
            total_ref[at] += dot(pre_low, up_ref[...], 1, 1)
        @each(row_tiles(width, width // 2))
        def _(at):
            up_g[at] = dot(normed_t[at], pre_ref[...], 1, 0).astype(BF16)

    by_half(
        steps,
        lambda: run(up_own, down_own, slope_own, up_g_own),
        lambda: run(up_oth, down_oth, slope_oth, up_g_oth),
    )

    @pl.when(index == 2 * steps - 1)
    def _():
        finish_rows(
            tiles, result_grad, resid_ref, total_ref, gain_ref, out_own, out_oth, attn_ref, mgrad_ref, gain_grad_ref
        )


def late_part(x, mixed, cot, spread, out_pair, gains, up_pair, down_pair, slope_pair, tile=512, chunk=768):
    rows, width = x.shape
    local_ff = up_pair[0].shape[1]
    steps = local_ff // chunk
    shape = jax.ShapeDtypeStruct
    cols = lambda height: [first_cols(height, chunk, steps), second_cols(height, chunk, steps)]
    return pl.pallas_call(
        functools.partial(late_kernel, tile=tile, steps=steps),
        grid=(2 * steps,),
        in_specs=[once(x), once(mixed), once(cot), once(spread), once(out_pair[0]), once(out_pair[1]), once(gains)]
        + cols(width) * 2
        + cols(rows),
        out_specs=[once(x), once(x), whole_shape((8, width))] + cols(width),
        out_shape=[shape((rows, width), BF16)] * 2 + [shape((8, width), F32)] + [shape((width, local_ff), BF16)] * 2,
        scratch_shapes=[
            pltpu.VMEM((width, rows), BF16),
            pltpu.VMEM((rows, width), BF16),
            pltpu.VMEM((rows, width), F32),
            pltpu.VMEM((rows, width), F32),
            pltpu.VMEM((rows, chunk), BF16),
        ],
        compiler_params=params(48),
        cost_estimate=cost(4 * rows * width * (width + 3 * local_ff), rows * (width * 10 + local_ff * 4) + width * (width + local_ff * 6) * 2),
        name="late_part",
    )(x, mixed, cot, spread, *out_pair, gains, *up_pair, *down_pair, *slope_pair)


def blank(*likes):
    return pl.pallas_call(
        lambda *refs: None,
        out_specs=[pl.BlockSpec(memory_space=pl.ANY)] * len(likes),
        out_shape=[jax.ShapeDtypeStruct(shape, dtype) for shape, dtype in likes],
        compiler_params=params(4),
        name="blank",
    )()


def input_kernel(
    x_ref, normed_ref, attn_ref, mixed_ref, d_own, d_oth, w_own, w_oth, gain_ref,
    out_ref, gain_grad_ref, g_own, g_oth, total_ref, normed_t, attn_t, *, tile, steps
):
    index = pl.program_id(0)
    width = x_ref.shape[1]
    half = width // 2
    tiles = row_tiles(x_ref.shape[0], tile)

    @pl.when(index == 0)
    def _():
        total_ref[...] = jnp.zeros_like(total_ref)
        @each(tiles, True)
        def _(at):
            normed_t[:, at] = normed_ref[at].T
            attn_t[:, at] = attn_ref[at].T

    def run(d_ref, w_ref, g_ref):
        @each(tiles, True)
        def _(at):
            total_ref[at] += dot(d_ref[at], w_ref[...], 1, 1)
        @each(row_tiles(width, width // 3), True)
        def _(at):
            g_ref[at] = dot(normed_t[at], d_ref[...], 1, 0).astype(BF16)

    def run_out(cols, g_ref):
        @each(row_tiles(width, width // 3), True)
        def _(at):
            g_ref[at] = dot(attn_t[at], mixed_ref[:, cols], 1, 0).astype(BF16)

    pl.when(index < steps)(lambda: run(d_own, w_own, g_own))
    pl.when(index == steps)(lambda: run_out(slice(0, half), g_own))
    pl.when((index > steps) & (index <= 2 * steps))(lambda: run(d_oth, w_oth, g_oth))

    @pl.when(index == 2 * steps + 1)
    def _():
        run_out(slice(half, width), g_oth)
        gain_grad_ref[...] = jnp.zeros_like(gain_grad_ref)

        @each(tiles, True)
        def _(at):
            part, gain_part = norm_back(x_ref[at].astype(F32), total_ref[at], gain_ref[0:1])
            gain_grad_ref[0:1] += gain_part
            out_ref[at] = (attn_ref[at].astype(F32) + part).astype(BF16)


def input_back(x, normed, attn_low, mixed, d_pair, w_pair, gains, tile=256):
    rows, width = x.shape
    wide = d_pair[0].shape[1]
    chunk = width // 2
    steps = wide // chunk
    shape = jax.ShapeDtypeStruct
    at_own = lambda height: pl.BlockSpec((height, chunk), lambda i: (0, jnp.minimum(i, steps - 1)))
    at_oth = lambda height: pl.BlockSpec((height, chunk), lambda i: (0, jnp.clip(i - steps - 1, 0, steps - 1)))
    return pl.pallas_call(
        functools.partial(input_kernel, tile=tile, steps=steps),
        grid=(2 * steps + 2,),
        in_specs=[once(x), once(x), once(x), once(x), at_own(rows), at_oth(rows), at_own(width), at_oth(width), once(gains)],
        out_specs=[once(x), whole_shape((8, width)), first_cols(width, chunk, steps + 1), second_cols(width, chunk, steps + 1)],
        out_shape=[shape((rows, width), BF16), shape((8, width), F32)] + [shape((width, wide + chunk), BF16)] * 2,
        scratch_shapes=[
            pltpu.VMEM((rows, width), F32),
            pltpu.VMEM((width, rows), BF16),
            pltpu.VMEM((width, rows), BF16),
        ],
        compiler_params=params(32),
        cost_estimate=cost(8 * rows * width * wide + 2 * rows * width * width, rows * (width * 10 + wide * 4) + width * wide * 8),
        name="qkv_back",
    )(x, normed, attn_low, mixed, *d_pair, *w_pair, gains)


def crossed():
    return lax.axis_index("half") != lax.axis_index("mp")


def swap_in(value):
    return lax.ppermute(value, ("half", "mp"), [(1, 2), (2, 1)])


def swapped(value):
    return jnp.where(crossed(), swap_in(value), value)


def from_mate(value):
    return lax.ppermute(value, "half", [(0, 1), (1, 0)])


def along_dp(value, bit):
    return lax.ppermute(value, "dp", [(i, i ^ bit) for i in range(8)])


def pick(value, index, axis=0):
    return lax.dynamic_index_in_dim(value, index, axis, keepdims=False)


def neighbours_swap(value):
    shards, split = lax.axis_size("dp"), lax.axis_size("mp")
    pairs = [
        ((h * shards + d) * split + m, (h * shards + (d ^ 1)) * split + m)
        for h in range(2)
        for d in range(shards)
        for m in range(split)
        if h != m
    ]
    return lax.ppermute(value, ("half", "dp", "mp"), pairs)


def after(value, *others):
    return lax.optimization_barrier((value, *others))[0]


def fetch(weight, gate=None, mate_gate=None):
    received = swap_in(weight if gate is None else after(weight, gate))
    own = jnp.where(crossed(), received if mate_gate is None else after(received, mate_gate), weight)
    return own, from_mate(own), received


def fetch_shared(weight, gate, pass_gate):
    rows, cols = weight.shape
    parts = weight.reshape(2, rows // 2, cols)
    odd = lax.axis_index("dp") % 2
    mine = swap_in(after(pick(parts, odd), gate))
    other = neighbours_swap(after(mine, pass_gate))
    got = jnp.where(odd == 0, jnp.stack([mine, other]), jnp.stack([other, mine]))
    own = jnp.where(crossed(), got, parts).reshape(rows, cols)
    return own, from_mate(own), mine


def low_sum(one, two):
    return (one.astype(F32) + two.astype(F32)).astype(BF16)


def by_place(grad):
    return grad.reshape(2, 2, 2, grad.shape[0] // 8, grad.shape[1])


def pair_summed(part, bit, axis, *gate):
    at = lax.axis_index("dp") // bit % 2
    got = along_dp(after(pick(part, 1 - at, axis), *gate), bit)
    return low_sum(pick(part, at, axis), got)


def x_summed(part, *gate):
    return pair_summed(part, 1, part.ndim - 3, *gate)


def z_summed(part, *gate):
    return pair_summed(pair_summed(part, 2, 1), 4, 0, *gate)


def all_sum(value):
    shards = lax.axis_size("dp")
    if shards != 8:
        return lax.psum(value, ("half", "dp"))
    value = value + from_mate(value)
    for bit in (1, 2, 4):
        value = value + along_dp(value, bit)
    return value


def body(tokens, norm_gains, qkv_w, out_w, up_w, down_w, memory, memory_ids, counts, prefix_mask, cotangent):
    core = lax.axis_index("half")
    layer = lax.axis_index("mp")
    shard_count = lax.axis_size("dp")
    shard_index = lax.axis_index("dp")
    rows, width = tokens.shape[1:]
    questions, k_most = memory_ids.shape
    mem_dev = memory.shape[1]
    score_scale = (4 * width) ** (-0.5)
    local_hd = qkv_w.shape[3]
    padded = 16

    gains = swapped(norm_gains[0])
    x_in = swap_in(tokens[0])
    x = jnp.where(crossed(), x_in, tokens[0])
    *qkv_pair, qkv_in = fetch(qkv_w[0].reshape(width, 3 * local_hd))
    normed, *proj = project(x, gains, qkv_pair)
    *out_pair, _ = fetch(out_w[0], qkv_in, proj[0])
    *up_pair, up_in = fetch_shared(up_w[0], x_in, proj[0])
    self_mixed = attention(*proj)
    *down_pair, down_in = fetch(down_w[0], qkv_in, self_mixed)
    cot = swapped(after(cotangent[0], down_in))

    slot_total = questions * k_most
    capacity = (slot_total + shard_count - 1) // shard_count
    table = memory[0].reshape(mem_dev, 4 * width)
    local_rows = jnp.concatenate(
        [memory_ids.reshape(-1) % mem_dev, jnp.zeros((capacity * shard_count - slot_total,), jnp.int32)]
    )
    requests = jnp.roll(local_rows.reshape(capacity, shard_count), shard_index, axis=1).T
    asked = lax.all_to_all(requests, "dp", split_axis=0, concat_axis=0, tiled=True).reshape(-1)
    answer = dot((asked[:, None] == jnp.arange(mem_dev)[None, :]).astype(BF16), table, 1, 0).astype(BF16)
    answers = lax.all_to_all(answer, "dp", split_axis=0, concat_axis=0, tiled=True)
    answers = swapped(after(answers, up_in))
    at = jnp.arange(questions * padded)
    slot = at % padded
    flat = at // padded * k_most + slot
    source = (shard_index + flat % shard_count) % shard_count * capacity + flat // shard_count
    source = jnp.where(slot < k_most, source, -1)
    chosen = (source[:, None] == jnp.arange(capacity * shard_count)[None, :]).astype(BF16)
    found = dot(chosen, answers, 1, 0).astype(BF16)
    half = width // 2
    other_way = jnp.concatenate(
        [found[:, c * width + h * half : c * width + (h + 1) * half] for c in range(4) for h in (1, 0)], axis=1
    )
    found_heads = jnp.where(core == 0, found, other_way).reshape(questions, padded, 4 * width)
    found = found.reshape(questions, padded, 4 * width)

    valid = (jnp.arange(k_most)[None, :] < counts[:, None])[:, None, :] & (
        jnp.swapaxes(prefix_mask.reshape(questions, k_most, 2), 1, 2) == 1
    )
    valid = jnp.pad(valid.astype(F32), ((0, 0), (0, 0), (0, padded - k_most))).reshape(questions, 2 * padded)
    valid = (swapped(valid) > 0.5) & (layer == 1)

    def biases(scores):
        wide = jnp.tile(jnp.pad(scores.astype(F32), ((0, 0), (0, padded - k_most))), (1, 2))
        bias = jnp.where(valid, wide, MASKED)
        return jnp.broadcast_to(bias[:, :, None], (questions, 2 * padded, LANES))

    joining = layer == 1
    pooled = pooled_result(x, self_mixed, out_pair, gains, up_pair, down_pair)
    pooled = (pooled * (1.0 / RUN)).reshape(questions, 4 * width)
    scores = jnp.sum(pooled[:, None, :] * found[:, :k_most].astype(F32), axis=-1) * score_scale
    sent = lax.ppermute(scores.astype(BF16), "mp", [(0, 1)])

    bias = biases(sent)
    local_ff = up_w.shape[2]
    tall = ((rows, local_ff), BF16)
    flat = ((rows, width), BF16)
    grad_like = ((width, local_ff), BF16)
    run_like = ((rows // RUN, local_ff), BF16)
    slot_like = ((questions, 2 * padded, LANES), F32)
    gain_like = ((8, width), F32)

    def join_first():
        mixed = attention(*proj, (found_heads, bias))
        attn_low, mgrad, gain_two, hid_own, hid_oth, pre_own, pre_oth = join_part(
            x, mixed, cot, out_pair, gains, up_pair, down_pair
        )
        slots = slot_sums(*proj, found_heads, bias, mgrad)
        unused = blank(grad_like, grad_like, run_like, run_like)
        return mixed, attn_low, mgrad, gain_two, hid_own, hid_oth, pre_own, pre_oth, slots, *unused

    def key_first():
        result, slope_own, slope_oth, *rest = early_part(x, self_mixed, cot, out_pair, gains, up_pair, down_pair)
        mgrad, gain_two, pre_own, pre_oth, slots = blank(flat, gain_like, tall, tall, slot_like)
        return self_mixed, result, mgrad, gain_two, slope_own, slope_oth, pre_own, pre_oth, slots, *rest

    (mixed, flat_one, mgrad, gain_two, tall_own, tall_oth, pre_own, pre_oth, slots, *key_down, run_own, run_oth) = lax.cond(
        joining, join_first, key_first
    )
    slot_grad = slots[:, :, 0]
    score_low = (slot_grad[:, :k_most] + slot_grad[:, padded : padded + k_most]).astype(BF16)
    score_in = lax.ppermute(score_low, "mp", [(1, 0)])

    scale = score_scale / RUN
    spread = jnp.sum(
        (score_in.astype(F32) * scale)[:, :, None] * found[:, :k_most].astype(F32), axis=1
    ).reshape(rows // RUN, width)

    def weight_grad(rows_of, cols_of, base=0.0):
        return (dot(rows_of, cols_of, 0, 0) + base).astype(BF16)

    def join_down():
        return lax.optimization_barrier((weight_grad(cot, tall_own), weight_grad(cot, tall_oth)))

    def key_down_all():
        spread_low = spread.astype(BF16)
        return lax.optimization_barrier(
            tuple(weight_grad(spread_low, r, g.astype(F32)) for g, r in zip(key_down, (run_own, run_oth)))
        )

    down_own, down_oth = lax.cond(joining, join_down, key_down_all)
    down_grad = low_sum(down_own, from_mate(down_oth))

    def join_second():
        result, up_own, up_oth = join_grads(
            x, mixed, out_pair, gains, down_pair, (tall_own, tall_oth), (pre_own, pre_oth)
        )
        return result, flat_one, mgrad, gain_two, up_own, up_oth

    def key_second():
        return flat_one, *late_part(
            x, mixed, cot, spread, out_pair, gains, up_pair, down_pair, (tall_own, tall_oth)
        )

    result, attn_low, mgrad, gain_two, up_own, up_oth = lax.cond(joining, join_second, key_second)
    ring = shard_count == 8
    down_part = x_summed(by_place(down_grad)) if ring else down_grad
    up_grad = low_sum(up_own, from_mate(after(up_oth, down_part)))
    d_own, d_oth, _ = attention_back(*proj, found_heads, bias, mgrad)
    result_in = swap_in(result)
    down_near = far = ()
    if ring:
        up_part = x_summed(by_place(up_grad))
        down_near = (pair_summed(down_part, 2, 1),)
        far = (pair_summed(down_near[0], 4, 0), up_part, result_in)
    grad_in, gain_one, head_own, head_oth = input_back(
        x, normed, attn_low, mixed, (after(d_own, up_grad, *down_near), d_oth), qkv_pair, gains
    )
    grad_in_recv = swap_in(grad_in)
    small = all_sum(after(jnp.concatenate([gain_one[:1], gain_two[:1]], axis=0), *far))
    head_grad = low_sum(head_own, after(from_mate(after(head_oth, *far)), small))

    def placed(sum_rows):
        return swapped(sum_rows.astype(BF16)).astype(F32)

    if ring:
        first, second = jnp.split(by_place(head_grad), 2, axis=-1)
        second = pair_summed(second, 2, 1)
        first = x_summed(first)
        up_near = pair_summed(up_part, 2, 1, second)
        second = pair_summed(second, 4, 0)
        down_g, up_g = placed(after(far[0], second)), placed(pair_summed(up_near, 4, 0))
        head_g = placed(jnp.concatenate([z_summed(first), x_summed(second)], axis=-1))
    else:
        down_g, up_g, head_g = (
            placed(lax.psum_scatter(g.astype(F32), "dp", scatter_dimension=0, tiled=True))
            for g in (down_part, up_grad, head_grad)
        )
    score_out = jnp.where(joining, score_low, score_in).astype(F32)
    score_out = jnp.pad(score_out.reshape(-1), (0, width - slot_total))[None]
    small = swapped(after(jnp.concatenate([small, score_out]), grad_in_recv, second if ring else head_grad))
    gain_grads, score_out = small[:2], small[2, :slot_total].reshape(questions, k_most)
    activations = jnp.where(crossed(), result_in, result)
    input_grad = jnp.where(crossed(), after(grad_in_recv, first) if ring else grad_in_recv, grad_in).astype(F32)
    return (
        activations[None],
        input_grad[None],
        score_out,
        gain_grads[None],
        head_g[:, : 3 * local_hd].reshape(1, -1, 3, local_hd),
        head_g[None, :, 3 * local_hd :],
        up_g[None],
        down_g[None],
    )


def solution(mesh):
    placed = (
        P("half", ("dp", "mp"), None),
        P("half", None, None),
        P("half", None, None, "mp"),
        P("half", None, "mp"),
        P("half", None, "mp"),
        P("half", None, "mp"),
        P("half", "dp", None, None),
        P(("dp", "mp"), None),
        P(("dp", "mp")),
        P(("dp", "mp"), None),
        P("half", ("dp", "mp"), None),
    )
    return jax.shard_map(
        body,
        mesh=mesh,
        in_specs=placed,
        out_specs=(
            P("half", ("dp", "mp"), None),
            P("half", ("dp", "mp"), None),
            P(("dp", "mp"), None),
            P("half", None, None),
            P("half", "dp", None, "mp"),
            P("half", "dp", "mp"),
            P("half", "dp", "mp"),
            P("half", "dp", "mp"),
        ),
        check_vma=False,
    )
```
